32 devices in a mesh: res: 8 (over y, x, core), tp: 4 (over z).
Axes of the slice: x: 2, y: 2, z: 4, core: 2. Of those that a mesh axis runs over, the one named last changes fastest.
Arguments:
- node_feats: bfloat16 [2, 4096, 512], P(None, ('res', 'tp')), may hold values from -6 to 6
- edge_feats: bfloat16 [2, 4096, 60, 192], P(None, ('res', 'tp')), may hold values from -6 to 6
- slot_index: int32 [2, 4096, 60], P(None, ('res', 'tp')), may hold values from 0 to 511, as said below
- send_rows: int32 [2, 32, 32, 16], P(None, ('res', 'tp')), may hold values from 0 to 127, as said below
- res_mask: int32 [2, 4096], P(None, ('res', 'tp')), may hold values 0 or 1
- chain_ids: int32 [2, 4096], P(None, ('res', 'tp')), may hold values from 0 to 15, never falling along the last dimension, each value on 1 to 512 neighbouring positions
- node_upstream: bfloat16 [2, 4096, 512], P(None, ('res', 'tp')), may hold values from -6 to 6
- edge_upstream: bfloat16 [2, 4096, 60, 192], P(None, ('res', 'tp')), may hold values from -6 to 6
- message_square: float32 [4, 512, 512], P(None, 'tp'), may hold values from -0.25 to 0.25
- message_edge: float32 [192, 512], P('tp'), may hold values from -0.4375 to 0.4375
- expand_weight: float32 [512, 2048], P('tp'), may hold values from -0.25 to 0.25
- contract_weight: float32 [2048, 512], P('tp'), may hold values from -0.125 to 0.125
- edge_input: float32 [2, 512, 192], P(None, 'tp'), may hold values from -0.25 to 0.25
- edge_square: float32 [3, 192, 192], P(None, 'tp'), may hold values from -0.4375 to 0.4375
- gains_biases: float32 [8256], P('tp')
- message_square_first: float32 [4, 512, 512], P(None, 'tp'), may hold values from -0.0034179688 to 0.0034179688
- message_edge_first: float32 [192, 512], P('tp'), may hold values from -0.00048828125 to 0.00048828125
- expand_weight_first: float32 [512, 2048], P('tp'), may hold values from -0.0034179688 to 0.0034179688
- contract_weight_first: float32 [2048, 512], P('tp'), may hold values from -0.0034179688 to 0.0034179688
- edge_input_first: float32 [2, 512, 192], P(None, 'tp'), may hold values from -0.0034179688 to 0.0034179688
- edge_square_first: float32 [3, 192, 192], P(None, 'tp'), may hold values from -0.0034179688 to 0.0034179688
- gains_biases_first: float32 [8256], P('tp'), may hold values from -0.009765625 to 0.009765625
- message_square_second: float32 [4, 512, 512], P(None, 'tp'), may hold values from 2.8093928e-07 to 1.1237571e-06
- message_edge_second: float32 [192, 512], P('tp'), may hold values from 3.9019343e-09 to 1.5607737e-08
- expand_weight_second: float32 [512, 2048], P('tp'), may hold values from 2.8093928e-07 to 1.1237571e-06
- contract_weight_second: float32 [2048, 512], P('tp'), may hold values from 2.8093928e-07 to 1.1237571e-06
- edge_input_second: float32 [2, 512, 192], P(None, 'tp'), may hold values from 2.8093928e-07 to 1.1237571e-06
- edge_square_second: float32 [3, 192, 192], P(None, 'tp'), may hold values from 2.8093928e-07 to 1.1237571e-06
- gains_biases_second: float32 [8256], P('tp'), may hold values from 2.5284535e-06 to 1.0113814e-05
Outputs:
- node_out: float32 [2, 4096, 512], P(None, ('res', 'tp'))
- edge_out: float32 [2, 4096, 60, 192], P(None, ('res', 'tp'))
- node_grad: float32 [2, 4096, 512], P(None, ('res', 'tp'))
- edge_grad: float32 [2, 4096, 60, 192], P(None, ('res', 'tp'))
- grad_norm: float32 [1], replicated
- new_message_square: float32 [4, 512, 512], P(None, 'tp')
- new_message_edge: float32 [192, 512], P('tp')
- new_expand_weight: float32 [512, 2048], P('tp')
- new_contract_weight: float32 [2048, 512], P('tp')
- new_edge_input: float32 [2, 512, 192], P(None, 'tp')
- new_edge_square: float32 [3, 192, 192], P(None, 'tp')
- new_gains_biases: float32 [8256], P('tp')
- new_message_square_first: float32 [4, 512, 512], P(None, 'tp')
- new_message_edge_first: float32 [192, 512], P('tp')
- new_expand_weight_first: float32 [512, 2048], P('tp')
- new_contract_weight_first: float32 [2048, 512], P('tp')
- new_edge_input_first: float32 [2, 512, 192], P(None, 'tp')
- new_edge_square_first: float32 [3, 192, 192], P(None, 'tp')
- new_gains_biases_first: float32 [8256], P('tp')
- new_message_square_second: float32 [4, 512, 512], P(None, 'tp')
- new_message_edge_second: float32 [192, 512], P('tp')
- new_expand_weight_second: float32 [512, 2048], P('tp')
- new_contract_weight_second: float32 [2048, 512], P('tp')
- new_edge_input_second: float32 [2, 512, 192], P(None, 'tp')
- new_edge_square_second: float32 [3, 192, 192], P(None, 'tp')
- new_gains_biases_second: float32 [8256], P('tp')
The draws below stay inside these ranges and needn't reach their ends.
Inputs may be any that keep to these rules, and one draw needn't show every extreme that they name: slot_index = s * 16 + c names the row send_rows[m, s, d, c] of device s, d being the device of the edge's residue. `send_rows`: the 16 rows that one device sends to one device are distinct. `chain_ids`: ids never fall along the residues of a micro-batch.
All inputs are finite; a program needn't handle non-finite values. No bound on the sum of `res_mask` on one device may be relied on, other than what follows from the above.
Results may differ from the reference program's by a relative error of at most 0.012.
The reference program's roundings to bfloat16 on the way count: a program that leaves them out, or rounds other values in their place, can miss the bound.
Values may be sent and summed in bfloat16 or wider, within the bound.
A program may use at most 384 MiB of HBM per device.

```python
import math
import jax
import jax.numpy as jnp
import numpy as np
from jax import lax

D = 512
E = 192
F = 2048
K = 60
NODE_DEV = 128
CAP = 16
MB = 2
STEP = 5
DEVS = 32
RES = 4096
VEC = 8256
PARAMS = 3559488


def draw_send_rows(key, part):
    scores = jax.random.randint(key, (MB, DEVS, DEVS, NODE_DEV), 0, 1048576)
    scores = scores * NODE_DEV + jnp.arange(NODE_DEV, dtype=jnp.int32)
    ranked = jnp.argsort(scores, axis=-1)
    return ranked[..., :CAP].astype(jnp.int32)


def draw_slot_index(key, part):
    first_key, second_key, third_key = jax.random.split(key, 3)
    draw_shape = (MB, RES, K)
    owner_dev = (jnp.arange(RES, dtype=jnp.int32) // NODE_DEV)[None, :, None]
    offset = jax.random.randint(first_key, draw_shape, -1, 2)
    near_source = (owner_dev + offset) % DEVS
    far_source = jax.random.randint(second_key, draw_shape, 0, DEVS)
    position = jnp.arange(K, dtype=jnp.int32)[None, None, :]
    source = jnp.where(position < K // 3, near_source, far_source)
    column = jax.random.randint(third_key, draw_shape, 0, CAP)
    return (source * CAP + column).astype(jnp.int32)


def draw_gains_biases(key, part):
    normal_draw = jax.random.normal(key, (VEC,), jnp.float32)
    position = jnp.arange(VEC)
    is_gain = (position < 6 * D) & (position // D % 2 == 0)
    return jnp.where(is_gain, 1.0 + 0.15 * normal_draw, 0.2 * normal_draw).astype(jnp.float32)


def touch_ends(entries, key, low, high):
    extent = entries.shape
    index_at = [jax.random.randint(jax.random.fold_in(key, axis), (), 0, extent[axis]) for axis in range(len(extent))]
    entries = entries.at[tuple(index_at)].set(low)
    longest = extent.index(max(extent))
    index_at[longest] = (index_at[longest] + 1) % extent[longest]
    return entries.at[tuple(index_at)].set(high)


def block_levels(stream_key, dims, cuts, least, top_value):
    factor_of = 1.0
    for axis_at, parts in cuts:
        draws = jax.random.uniform(jax.random.fold_in(jax.random.fold_in(stream_key, 6), axis_at), (parts,), jnp.float32, least / len(cuts), top_value / len(cuts))
        factor_of = factor_of * jnp.repeat(jnp.exp(draws), dims[axis_at] // parts).reshape((-1,) + (1,) * (len(dims) - 1 - axis_at))
    return factor_of


def profile(number_of, total, limit, slope):
    loads = [(1 << 20) // math.isqrt(standing ** slope) + 1 for standing in range(2, number_of + 1)]
    rest, holding = total - limit - (number_of - 1), [1] * (number_of - 1)
    while rest > 0:
        candidates = [i for i in range(number_of - 1) if holding[i] < limit]
        whole, remaining = sum([loads[i] for i in candidates]), rest
        for i in candidates:
            extra = min(limit - holding[i], max(1, remaining * loads[i] // whole), rest)
            holding[i] = holding[i] + extra
            rest = rest - extra
    return np.array([limit] + holding)


def ragged_sizes(own_key, number_of, total, bound, skew):
    if number_of == 2:
        one = jax.random.randint(own_key, (), max(1, total - bound), min(bound, total - 1) + 1)
        return jnp.stack([one, total - one])
    lengths = jnp.asarray(profile(number_of, total, bound, skew), jnp.int32)
    twos = (number_of - 1) // 2
    source_of, taker = lengths[1:1 + 2 * twos:2], lengths[2:2 + 2 * twos:2]
    margin = jnp.minimum(source_of - 1, bound - taker)
    passed = jax.random.randint(jax.random.fold_in(own_key, 1), (twos,), 0, 1 << 20) % (margin + 1)
    lengths = lengths.at[1:1 + 2 * twos:2].set(source_of - passed).at[2:2 + 2 * twos:2].set(taker + passed)
    return lengths[jax.random.permutation(jax.random.fold_in(own_key, 2), number_of)]


def bell_draw(key, dims, deviation, bound, cuts=(), kind=jnp.bfloat16):
    drawn = deviation * jax.random.normal(key, dims, jnp.float32)
    if cuts:
        drawn = drawn * block_levels(key, dims, cuts, -0.22, 0.18)
    return jnp.clip(drawn, -bound, bound).astype(kind)


def setup_inputs(seed: int = 0) -> dict:
    arg_keys = jax.random.split(jax.random.key(seed), 30)
    node_feats = bell_draw(arg_keys[0], (MB, RES, D), 1.0, 6.0, ((1, 32),))
    edge_feats = bell_draw(arg_keys[1], (MB, RES, K, E), 1.0, 6.0, ((1, 32),))
    slot_index = draw_slot_index(jax.random.fold_in(arg_keys[29], 71), 0)
    send_rows = draw_send_rows(jax.random.fold_in(arg_keys[29], 71), 0)
    res_mask = touch_ends((jax.random.randint(arg_keys[4], (MB, RES), 0, 10) < 9).astype(jnp.int32), jax.random.fold_in(arg_keys[4], 1), 0, 1)
    chain_ids = jax.vmap(lambda own: jnp.searchsorted(jnp.cumsum(ragged_sizes(own, 16, RES, RES // 8, 0)), jnp.arange(RES), side="right"))(jax.random.split(arg_keys[5], MB)).reshape((MB, RES)).astype(jnp.int32)
    node_upstream = bell_draw(arg_keys[6], (MB, RES, D), 1.0, 6.0, ((1, 32),))
    edge_upstream = bell_draw(arg_keys[7], (MB, RES, K, E), 1.0, 6.0, ((1, 32),))
    message_square = bell_draw(arg_keys[8], (4, D, D), D ** -0.5, 0.25, ((1, 4),), jnp.float32)
    message_edge = bell_draw(arg_keys[9], (E, D), E ** -0.5, 0.4375, ((0, 4),), jnp.float32)
    expand_weight = bell_draw(arg_keys[10], (D, F), D ** -0.5, 0.25, ((0, 4),), jnp.float32)
    contract_weight = bell_draw(arg_keys[11], (F, D), F ** -0.5, 0.125, ((0, 4),), jnp.float32)
    edge_input = bell_draw(arg_keys[12], (2, D, E), D ** -0.5, 0.25, ((1, 4),), jnp.float32)
    edge_square = bell_draw(arg_keys[13], (3, E, E), E ** -0.5, 0.4375, ((1, 4),), jnp.float32)
    gains_biases = draw_gains_biases(jax.random.fold_in(arg_keys[29], 71), 0)
    message_square_first = bell_draw(arg_keys[15], (4, D, D), (PARAMS ** -0.5), 0.0034179688, ((1, 4),), jnp.float32)
    message_edge_first = bell_draw(arg_keys[16], (E, D), (9.0 / K * PARAMS ** -0.5), 0.00048828125, ((0, 4),), jnp.float32)
    expand_weight_first = bell_draw(arg_keys[17], (D, F), (PARAMS ** -0.5), 0.0034179688, ((0, 4),), jnp.float32)
    contract_weight_first = bell_draw(arg_keys[18], (F, D), (PARAMS ** -0.5), 0.0034179688, ((0, 4),), jnp.float32)
    edge_input_first = bell_draw(arg_keys[19], (2, D, E), (PARAMS ** -0.5), 0.0034179688, ((1, 4),), jnp.float32)
    edge_square_first = bell_draw(arg_keys[20], (3, E, E), (PARAMS ** -0.5), 0.0034179688, ((1, 4),), jnp.float32)
    gains_biases_first = bell_draw(arg_keys[21], (VEC,), (3 * PARAMS ** -0.5), 0.009765625, ((0, 4),), jnp.float32)
    message_square_second = jnp.clip(jnp.exp(math.log(1.1237571015954018e-06) - 1.3862944 * jax.random.uniform(arg_keys[22], (4, D, D), jnp.float32) ** block_levels(arg_keys[22], (4, D, D), ((1, 4),), -0.2, 0.2)), 2.8093927539885044e-07, 1.1237571015954018e-06)
    message_edge_second = jnp.clip(jnp.exp(math.log(1.5607737324785376e-08) - 1.3862944 * jax.random.uniform(arg_keys[23], (E, D), jnp.float32) ** block_levels(arg_keys[23], (E, D), ((0, 4),), -0.2, 0.2)), 3.901934331196344e-09, 1.5607737324785376e-08)
    expand_weight_second = jnp.clip(jnp.exp(math.log(1.1237571015954018e-06) - 1.3862944 * jax.random.uniform(arg_keys[24], (D, F), jnp.float32) ** block_levels(arg_keys[24], (D, F), ((0, 4),), -0.2, 0.2)), 2.8093927539885044e-07, 1.1237571015954018e-06)
    contract_weight_second = jnp.clip(jnp.exp(math.log(1.1237571015954018e-06) - 1.3862944 * jax.random.uniform(arg_keys[25], (F, D), jnp.float32) ** block_levels(arg_keys[25], (F, D), ((0, 4),), -0.2, 0.2)), 2.8093927539885044e-07, 1.1237571015954018e-06)
    edge_input_second = jnp.clip(jnp.exp(math.log(1.1237571015954018e-06) - 1.3862944 * jax.random.uniform(arg_keys[26], (2, D, E), jnp.float32) ** block_levels(arg_keys[26], (2, D, E), ((1, 4),), -0.2, 0.2)), 2.8093927539885044e-07, 1.1237571015954018e-06)
    edge_square_second = jnp.clip(jnp.exp(math.log(1.1237571015954018e-06) - 1.3862944 * jax.random.uniform(arg_keys[27], (3, E, E), jnp.float32) ** block_levels(arg_keys[27], (3, E, E), ((1, 4),), -0.2, 0.2)), 2.8093927539885044e-07, 1.1237571015954018e-06)
    gains_biases_second = jnp.clip(jnp.exp(math.log(1.0113813914358616e-05) - 1.3862944 * jax.random.uniform(arg_keys[28], (VEC,), jnp.float32) ** block_levels(arg_keys[28], (VEC,), ((0, 4),), -0.2, 0.2)), 2.528453478589654e-06, 1.0113813914358616e-05)
    return dict(node_feats=node_feats, edge_feats=edge_feats, slot_index=slot_index, send_rows=send_rows, res_mask=res_mask, chain_ids=chain_ids, node_upstream=node_upstream, edge_upstream=edge_upstream, message_square=message_square, message_edge=message_edge, expand_weight=expand_weight, contract_weight=contract_weight, edge_input=edge_input, edge_square=edge_square, gains_biases=gains_biases, message_square_first=message_square_first, message_edge_first=message_edge_first, expand_weight_first=expand_weight_first, contract_weight_first=contract_weight_first, edge_input_first=edge_input_first, edge_square_first=edge_square_first, gains_biases_first=gains_biases_first, message_square_second=message_square_second, message_edge_second=message_edge_second, expand_weight_second=expand_weight_second, contract_weight_second=contract_weight_second, edge_input_second=edge_input_second, edge_square_second=edge_square_second, gains_biases_second=gains_biases_second)


@jax.custom_vjp
def low(v):
    return lax.optimization_barrier(v.astype(jnp.bfloat16)).astype(jnp.float32)

@jax.custom_vjp
def low_back(v):
    return v

def low_keep(v):
    return (low(v), None)

def low_pass(kept, grad):
    return (grad,)

def back_keep(v):
    return (v, None)

def back_low(kept, grad):
    return (low(grad),)
low.defvjp(low_keep, low_pass)
low_back.defvjp(back_keep, back_low)
norm_eps = 1e-05
learn_rate = 0.03
vector_rate = 0.25
beta_first = 0.5
beta_second = 0.5
adam_eps = 1e-08
decay_rate = 0.01
clip_norm = 1.0

def layer_norm(values, gain_row, shift_row):
    centred = values - lax.optimization_barrier(jnp.mean(values, axis=-1, keepdims=True))
    spread = lax.optimization_barrier(jnp.mean(centred * centred, axis=-1, keepdims=True))
    return centred * lax.rsqrt(spread + norm_eps) * gain_row + shift_row

def mix(left, weight):
    return jnp.einsum('nkd,dh->nkh', left, weight, precision=lax.Precision.HIGHEST)

def flat_dot(left, weight):
    return jnp.dot(left, weight, precision=lax.Precision.HIGHEST)

def adam_update(masters, firsts, seconds, grad_parts):
    square_sum = jnp.zeros((), jnp.float32)
    for grad_part in grad_parts:
        square_sum = square_sum + jnp.sum(grad_part * grad_part)
    grad_norm = jnp.sqrt(square_sum)
    clip_scale = clip_norm / jnp.maximum(grad_norm, clip_norm)
    first_fix = 1.0 - beta_first ** STEP
    second_fix = 1.0 - beta_second ** STEP
    decays = (decay_rate, decay_rate, decay_rate, decay_rate, decay_rate, decay_rate, 0.0)
    step_rates = (learn_rate, learn_rate, learn_rate, learn_rate, learn_rate, learn_rate, vector_rate)
    new_weights, new_firsts, new_seconds = ([], [], [])
    for master, first_moment, second_moment, grad_part, decay_now, rate_now in zip(masters, firsts, seconds, grad_parts, decays, step_rates):
        clipped = grad_part * clip_scale
        first_new = beta_first * first_moment + (1.0 - beta_first) * clipped
        second_new = beta_second * second_moment + (1.0 - beta_second) * clipped * clipped
        step_size = first_new / first_fix / (jnp.sqrt(second_new / second_fix) + adam_eps)
        new_weights.append(master - rate_now * (step_size + decay_now * master))
        new_firsts.append(first_new)
        new_seconds.append(second_new)
    return (grad_norm.reshape(1), new_weights, new_firsts, new_seconds)

def reference(node_feats, edge_feats, slot_index, send_rows, res_mask, chain_ids, node_upstream, edge_upstream, message_square, message_edge, expand_weight, contract_weight, edge_input, edge_square, gains_biases, message_square_first, message_edge_first, expand_weight_first, contract_weight_first, edge_input_first, edge_square_first, gains_biases_first, message_square_second, message_edge_second, expand_weight_second, contract_weight_second, edge_input_second, edge_square_second, gains_biases_second):
    total_rows = MB * RES
    blocks = total_rows // 256
    batch_ids = jnp.arange(MB, dtype=jnp.int32)[:, None, None]
    owner_dev = (jnp.arange(RES, dtype=jnp.int32) // NODE_DEV)[None, :, None]
    source = slot_index // CAP
    column = slot_index % CAP
    neighbour = source * NODE_DEV + send_rows[batch_ids, source, owner_dev, column]
    flat_neigh = (neighbour + batch_ids * RES).reshape(total_rows, K).astype(jnp.int32)
    mask_flat = res_mask.reshape(-1)
    chain_flat = chain_ids.reshape(-1)
    edge_valid = (mask_flat[:, None] * mask_flat[flat_neigh]).astype(jnp.float32)
    same_chain = (chain_flat[:, None] == chain_flat[flat_neigh]).astype(jnp.float32)
    neigh_count = jnp.maximum(lax.optimization_barrier(jnp.sum(edge_valid, axis=1)), 1.0)

    def forward(params, values_in, edge_in):
        rounded = tuple((low(param_item) for param_item in params))
        square, edge_proj, expand, contract, edge_proj_in, edge_sq, vector = rounded
        node_rows = vector[:11 * D].reshape(11, D)
        expand_bias = vector[11 * D:11 * D + F]
        edge_bias = vector[11 * D + F:].reshape(3, E)
        first_low = low(layer_norm(values_in, node_rows[0], node_rows[1]))
        self_term = flat_dot(first_low, square[0]) + node_rows[6]

        def message_block(pieces):
            neigh_block, edge_block, valid_block, same_block, self_block, count_block = pieces
            neigh_rows = first_low[neigh_block]
            pre_one = low_back(self_block[:, None, :] + mix(neigh_rows, square[1]) + mix(edge_block, edge_proj) + same_block[:, :, None] * node_rows[7])
            act_one = low(jax.nn.gelu(pre_one))
            pre_two = low_back(mix(act_one, square[2]) + node_rows[8])
            act_two = low(jax.nn.gelu(pre_two))
            message = low_back(mix(act_two, square[3]) + node_rows[9])
            return lax.optimization_barrier(jnp.sum(valid_block[:, :, None] * message, axis=1)) / count_block[:, None]
        pieces = (flat_neigh.reshape(blocks, -1, K), edge_in.reshape(blocks, -1, K, E), edge_valid.reshape(blocks, -1, K), same_chain.reshape(blocks, -1, K), self_term.reshape(blocks, -1, D), neigh_count.reshape(blocks, -1))
        gathered = lax.map(jax.checkpoint(message_block), pieces).reshape(total_rows, D)
        mixed_rows = values_in + gathered
        second_low = low(layer_norm(mixed_rows, node_rows[2], node_rows[3]))
        expand_pre = low_back(flat_dot(second_low, expand) + expand_bias)
        expand_act = low(jax.nn.gelu(expand_pre))
        node_out = mixed_rows + low_back(flat_dot(expand_act, contract) + node_rows[10])
        third_low = low(layer_norm(node_out, node_rows[4], node_rows[5]))
        edge_self = flat_dot(third_low, edge_proj_in[0]) + edge_bias[0]

        def edge_block_update(pieces):
            neigh_block, edge_block, valid_block, self_block = pieces
            neigh_rows = third_low[neigh_block]
            pre_one = low_back(self_block[:, None, :] + mix(neigh_rows, edge_proj_in[1]) + mix(edge_block, edge_sq[0]))
            act_one = low(jax.nn.gelu(pre_one))
            pre_two = low_back(mix(act_one, edge_sq[1]) + edge_bias[1])
            act_two = low(jax.nn.gelu(pre_two))
            delta = low_back(mix(act_two, edge_sq[2]) + edge_bias[2])
            return edge_block + valid_block[:, :, None] * delta
        edge_pieces = (flat_neigh.reshape(blocks, -1, K), edge_in.reshape(blocks, -1, K, E), edge_valid.reshape(blocks, -1, K), edge_self.reshape(blocks, -1, E))
        edge_out = lax.map(jax.checkpoint(edge_block_update), edge_pieces).reshape(total_rows, K, E)
        return (node_out, edge_out)
    params = (message_square, message_edge, expand_weight, contract_weight, edge_input, edge_square, gains_biases)
    values_in = node_feats.astype(jnp.float32).reshape(total_rows, D)
    edge_in = edge_feats.astype(jnp.float32).reshape(total_rows, K, E)
    outputs, pullback = jax.vjp(forward, params, values_in, edge_in)
    grad_parts, node_grad, edge_grad = pullback((node_upstream.astype(jnp.float32).reshape(total_rows, D), edge_upstream.astype(jnp.float32).reshape(total_rows, K, E)))
    firsts = (message_square_first, message_edge_first, expand_weight_first, contract_weight_first, edge_input_first, edge_square_first, gains_biases_first)
    seconds = (message_square_second, message_edge_second, expand_weight_second, contract_weight_second, edge_input_second, edge_square_second, gains_biases_second)
    grad_norm, new_weights, new_firsts, new_seconds = adam_update(params, firsts, seconds, grad_parts)
    return (outputs[0].reshape(MB, RES, D), outputs[1].reshape(MB, RES, K, E), node_grad.reshape(MB, RES, D), edge_grad.reshape(MB, RES, K, E), grad_norm, new_weights[0], new_weights[1], new_weights[2], new_weights[3], new_weights[4], new_weights[5], new_weights[6], new_firsts[0], new_firsts[1], new_firsts[2], new_firsts[3], new_firsts[4], new_firsts[5], new_firsts[6], new_seconds[0], new_seconds[1], new_seconds[2], new_seconds[3], new_seconds[4], new_seconds[5], new_seconds[6])
```

```python
import functools

import jax
import jax.numpy as jnp
from jax import lax
from jax.experimental import pallas as pl
from jax.experimental.pallas import tpu as pltpu
from jax.sharding import PartitionSpec as P

D = 512
E = 192
F = 2048
STEP = 5

norm_eps = 1e-05
learn_rate = 0.03
vector_rate = 0.25
beta_first = 0.5
beta_second = 0.5
adam_eps = 1e-08
decay_rate = 0.01
clip_norm = 1.0

C0 = 0.7978845608028654
C1 = C0 * 0.044715
bf16 = jnp.bfloat16
f32 = jnp.float32
VMEM_LIMIT = 58 * 1024 * 1024


def gelu_pair(z):
    q = z * z
    t = jnp.tanh(z * (q * C1 + C0))
    s = 0.5 * t + 0.5
    p = z * s
    d = s + (p - p * s) * (q * (6.0 * C1) + 2.0 * C0)
    return p, d


def dot(a, b):
    return jnp.dot(a, b, preferred_element_type=f32)


def dot_t(a, b):
    return lax.dot_general(a, b, (((1,), (1,)), ((), ())), preferred_element_type=f32)


def tdot(a, b):
    return lax.dot_general(a, b, (((0,), (0,)), ((), ())), preferred_element_type=f32)


def turned(v):
    n = v.shape[1]
    eye = lax.broadcasted_iota(jnp.int32, (n, n), 0) == lax.broadcasted_iota(jnp.int32, (n, n), 1)
    return dot_t(jnp.where(eye, 1.0, 0.0).astype(bf16), v)


def split2(v):
    hi = v.astype(bf16)
    lo = (v - hi.astype(f32)).astype(bf16)
    return hi, lo


def normed(v):
    centred = v - jnp.mean(v, axis=-1, keepdims=True)
    spread = jnp.mean(centred * centred, axis=-1, keepdims=True)
    rs = lax.rsqrt(spread + norm_eps)
    return centred * rs, rs


def norm_back(xhat, rs, gain, grad):
    gn = grad * gain
    gx = rs * (
        gn
        - jnp.mean(gn, axis=-1, keepdims=True)
        - xhat * jnp.mean(gn * xhat, axis=-1, keepdims=True)
    )
    return gx, jnp.sum(grad * xhat, axis=0, keepdims=True), jnp.sum(grad, axis=0, keepdims=True)


def whole(*dims):
    zero = (0,) * len(dims)
    return pl.BlockSpec(dims, lambda i: zero)


def picked(m, *dims):
    index = (m,) + (0,) * len(dims)
    return pl.BlockSpec((1,) + dims, lambda i: index)


def one_hots(slot, m, k0, count, S):
    n = slot.shape[2]
    iota = lax.broadcasted_iota(jnp.int32, (S, n), 0)
    return jnp.concatenate(
        [
            jnp.where(iota == slot[k0 + j, m : m + 1, :], 1.0, 0.0).astype(bf16)
            for j in range(count)
        ],
        axis=1,
    )


def wide(ref3, k0, count):
    return jnp.concatenate([ref3[k0 + j] for j in range(count)], axis=1)


def msg_fwd_body(
    m, KB, sub, S, slot, own, ef, tab, u1, wnbr, wself, wedge, w2, rows,
    p1o, d1o, d2o, pso, cnto, vso, tt_s, zs_s, zc_s, we_s, w2_s, c2_s,
):
    step = pl.program_id(0)
    N = ef.shape[3]

    @pl.when(step == 0)
    def _():
        tt_s[0:D, :] = dot(tab[0, :, 0:D], wnbr[0]).T.astype(bf16)
        tt_s[D:, :] = tab[0, :, D : D + 128].astype(f32).T[0:16, :].astype(bf16)
        zs = dot(u1[0], wself[0]) + rows[6:7, :]
        zs_s[...] = zs.T
        zc_s[...] = (zs + rows[7:8, :]).T
        we_s[...] = wedge[...].astype(f32).T.astype(bf16)
        w2_s[...] = w2[0].astype(f32).T.astype(bf16)
        c2_s[...] = jnp.broadcast_to(rows[8:9, :], (N, D)).T
        pso[...] = jnp.zeros_like(pso)
        cnto[...] = jnp.zeros_like(cnto)

    own_row = own[m : m + 1, :]
    FC = 128
    for s in range(KB // sub):
        k0 = s * sub
        oht = one_hots(slot, m, k0, sub, S)
        z1 = dot(tt_s[...], oht)
        ze = dot(we_s[...], jnp.concatenate([ef[0, k0 + j] for j in range(sub)], axis=1))
        vals = []
        parts = []
        for j in range(sub):
            k = k0 + j
            lo, hi = j * N, (j + 1) * N
            tag = z1[D : D + 1, lo:hi]
            v = jnp.where((tag > 0.0) & (own_row > 0.0), 1.0, 0.0)
            same = tag == own_row
            vals.append(v)
            vso[k, 0:1, :] = v
            vso[k, 1:2, :] = jnp.where(same, 1.0, 0.0)
            cnto[0:1, :] += v
            for c in range(0, D, FC):
                base = jnp.where(same, zc_s[c : c + FC, :], zs_s[c : c + FC, :])
                p, d = gelu_pair(z1[c : c + FC, lo:hi] + ze[c : c + FC, lo:hi] + base)
                p1o[k, c : c + FC, :] = p.astype(bf16)
                d1o[k, c : c + FC, :] = d.astype(bf16)
        z2 = dot(w2_s[...], wide(p1o, k0, sub))
        for j in range(sub):
            k = k0 + j
            lo, hi = j * N, (j + 1) * N
            for c in range(0, D, FC):
                p, d = gelu_pair(z2[c : c + FC, lo:hi] + c2_s[c : c + FC, :])
                d2o[k, c : c + FC, :] = (d * vals[j]).astype(bf16)
                pso[c : c + FC, :] += p * vals[j]


def msg_fwd(m, slot, own, ef, tab, u1, square, wedge, rows, KB=12, sub=6):
    K, N = ef.shape[1], ef.shape[3]
    S = tab.shape[1]
    return pl.pallas_call(
        functools.partial(msg_fwd_body, m, KB, sub, S),
        grid=(K // KB,),
        in_specs=[
            pl.BlockSpec((KB, 2, N), lambda i: (i, 0, 0)),
            whole(2, N),
            pl.BlockSpec((1, KB, E, N), lambda i: (m, i, 0, 0)),
            picked(0, S, D + 128),
            picked(m, N, D),
            picked(1, D, D),
            picked(0, D, D),
            whole(E, D),
            picked(2, D, D),
            whole(16, D),
        ],
        out_specs=[
            pl.BlockSpec((KB, D, N), lambda i: (i, 0, 0)),
            pl.BlockSpec((KB, D, N), lambda i: (i, 0, 0)),
            pl.BlockSpec((KB, D, N), lambda i: (i, 0, 0)),
            whole(D, N),
            whole(8, N),
            pl.BlockSpec((KB, 2, N), lambda i: (i, 0, 0)),
        ],
        out_shape=[
            jax.ShapeDtypeStruct((K, D, N), bf16),
            jax.ShapeDtypeStruct((K, D, N), bf16),
            jax.ShapeDtypeStruct((K, D, N), bf16),
            jax.ShapeDtypeStruct((D, N), f32),
            jax.ShapeDtypeStruct((8, N), f32),
            jax.ShapeDtypeStruct((K, 2, N), f32),
        ],
        scratch_shapes=[
            pltpu.VMEM((D + 16, S), bf16),
            pltpu.VMEM((D, N), f32),
            pltpu.VMEM((D, N), f32),
            pltpu.VMEM((D, E), bf16),
            pltpu.VMEM((D, D), bf16),
            pltpu.VMEM((D, N), f32),
        ],
        compiler_params=pltpu.CompilerParams(vmem_limit_bytes=VMEM_LIMIT),
        name="msg_fwd",
        cost_estimate=pl.CostEstimate(
            flops=2 * N * K * 10 * 65536, bytes_accessed=N * K * D * 6, transcendentals=0
        ),
    )(slot, own, ef, tab, u1, square, square, wedge, square, rows)


def edge_body(m, KB, sub, S, first, slot, vs, ef, up, tab, ys, vsq, rows, *refs):
    refs, scr = refs[:-10], refs[-10:]
    (eo, gy1o, gyso, so, dvo, dbo) = refs[-6:]
    (nt_s, vt_s, b_s, oh_s, r1_s, r2_s, g3_s, g2_s, ef_s, acc_s) = scr
    step = pl.program_id(0)
    N = ef.shape[3]

    @pl.when(step == 0)
    def _():
        nt_s[...] = turned(tab[...]).astype(bf16)
        for i in range(3):
            vt_s[i] = turned(vsq[i]).astype(bf16)
        for i in range(2):
            b_s[i] = jnp.broadcast_to(rows[i + 1 : i + 2, :], (N, E)).T
        gyso[...] = jnp.zeros_like(gyso)
        acc_s[...] = jnp.zeros_like(acc_s)
        if first:
            dvo[...] = jnp.zeros_like(dvo)
            dbo[...] = jnp.zeros_like(dbo)
        else:
            dvo[...] = refs[0][...]
            dbo[...] = refs[1][...]

    w = sub * N
    for s in range(KB // sub):
        k0 = s * sub
        lo = s * w
        oht = one_hots(slot, m, k0, sub, S)
        oh_s[:, lo : lo + w] = oht
        eft = jnp.concatenate([ef[0, k0 + j] for j in range(sub)], axis=1)
        ef_s[:, lo : lo + w] = eft
        base = jnp.concatenate([ys[...]] * sub, axis=1)
        r1, e1 = gelu_pair(dot(nt_s[...], oht) + dot(vt_s[0], eft) + base)
        r1 = r1.astype(bf16)
        r1_s[:, lo : lo + w] = r1
        r2, e2 = gelu_pair(dot(vt_s[1], r1) + jnp.concatenate([b_s[0]] * sub, axis=1))
        r2 = r2.astype(bf16)
        r2_s[:, lo : lo + w] = r2
        y3 = dot(vt_s[2], r2)
        for j in range(sub):
            v = vs[k0 + j, 0:1, :]
            eo[0, k0 + j] = ef[0, k0 + j].astype(f32) + v * (y3[:, j * N : (j + 1) * N] + b_s[1])
            g3f = v * up[0, k0 + j].astype(f32)
            acc_s[1] += g3f
            g3_s[:, lo + j * N : lo + (j + 1) * N] = g3f.astype(bf16)
        g2 = (e2 * dot(vsq[2], g3_s[:, lo : lo + w])).astype(bf16)
        g2_s[:, lo : lo + w] = g2
        g1 = (e1 * dot(vsq[1], g2)).astype(bf16)
        for j in range(sub):
            acc_s[0] += g2[:, j * N : (j + 1) * N].astype(f32)
            gyso[...] += g1[:, j * N : (j + 1) * N].astype(f32)
            gy1o[k0 + j] = g1[:, j * N : (j + 1) * N]
    g1 = wide(gy1o, 0, KB)
    part = dot_t(oh_s[...], g1)

    @pl.when(step == 0)
    def _():
        so[...] = part

    @pl.when(step > 0)
    def _():
        so[...] += part

    dvo[2] += dot_t(r2_s[...], g3_s[...])
    dvo[1] += dot_t(r1_s[...], g2_s[...])
    dvo[0] += dot_t(ef_s[...], g1)

    @pl.when(step == pl.num_programs(0) - 1)
    def _():
        dbo[1:2, :] += jnp.sum(acc_s[0].T, axis=0, keepdims=True)
        dbo[2:3, :] += jnp.sum(acc_s[1].T, axis=0, keepdims=True)


def edge_net(m, slot, vs, ef, up, tab, ys, vsq, rows, before, KB=12, sub=6):
    K, N = ef.shape[1], ef.shape[3]
    S = tab.shape[0]
    first = before is None
    extra = [] if first else list(before)
    args = [slot, vs, ef, up, tab, ys, vsq, rows]
    specs = [
        pl.BlockSpec((KB, 2, N), lambda i: (i, 0, 0)),
        pl.BlockSpec((KB, 2, N), lambda i: (i, 0, 0)),
        pl.BlockSpec((1, KB, E, N), lambda i: (m, i, 0, 0)),
        pl.BlockSpec((1, KB, E, N), lambda i: (m, i, 0, 0)),
        whole(S, E),
        whole(E, N),
        whole(3, E, E),
        whole(8, E),
    ]
    aliases = {}
    if not first:
        specs += [whole(3, E, E), whole(8, E), pl.BlockSpec(memory_space=pl.ANY)]
        aliases = {len(args) + 2: 0}
    L = KB * N
    return pl.pallas_call(
        functools.partial(edge_body, m, KB, sub, S, first),
        grid=(K // KB,),
        in_specs=specs,
        out_specs=[
            pl.BlockSpec((1, KB, E, N), lambda i: (m, i, 0, 0)),
            pl.BlockSpec((KB, E, N), lambda i: (i, 0, 0)),
            whole(E, N),
            whole(S, E),
            whole(3, E, E),
            whole(8, E),
        ],
        out_shape=[
            jax.ShapeDtypeStruct(ef.shape, f32),
            jax.ShapeDtypeStruct((K, E, N), bf16),
            jax.ShapeDtypeStruct((E, N), f32),
            jax.ShapeDtypeStruct((S, E), f32),
            jax.ShapeDtypeStruct((3, E, E), f32),
            jax.ShapeDtypeStruct((8, E), f32),
        ],
        scratch_shapes=[
            pltpu.VMEM((E, S), bf16),
            pltpu.VMEM((3, E, E), bf16),
            pltpu.VMEM((2, E, N), f32),
            pltpu.VMEM((S, L), bf16),
            pltpu.VMEM((E, L), bf16),
            pltpu.VMEM((E, L), bf16),
            pltpu.VMEM((E, L), bf16),
            pltpu.VMEM((E, L), bf16),
            pltpu.VMEM((E, L), bf16),
            pltpu.VMEM((2, E, N), f32),
        ],
        input_output_aliases=aliases,
        compiler_params=pltpu.CompilerParams(vmem_limit_bytes=VMEM_LIMIT),
        name="edge_net",
        cost_estimate=pl.CostEstimate(
            flops=2 * N * K * 12 * 65536, bytes_accessed=N * K * E * 12, transcendentals=0
        ),
    )(*args, *extra)


def msg_bwd_body(
    m, KB, sub, S, first, slot, vs, ef, up, p1, d1, d2, gy1, h, w2, wedge, vsq, *refs
):
    refs, scr = refs[:-4], refs[-4:]
    (ego, gzso, so, dw2o, dweo, dbo) = refs[-6:]
    (oh_s, g2_s, g1_s, acc_s) = scr
    step = pl.program_id(0)
    N = ef.shape[3]

    @pl.when(step == 0)
    def _():
        gzso[...] = jnp.zeros_like(gzso)
        acc_s[...] = jnp.zeros_like(acc_s)
        if first:
            dw2o[...] = jnp.zeros_like(dw2o)
            dweo[...] = jnp.zeros_like(dweo)
            dbo[...] = jnp.zeros_like(dbo)
        else:
            dw2o[...] = refs[0][...]
            dweo[...] = refs[1][...]
            dbo[...] = refs[2][...]

    w = sub * N
    FC = 128
    for s in range(KB // sub):
        k0 = s * sub
        lo = s * w
        oh_s[:, lo : lo + w] = one_hots(slot, m, k0, sub, S)
        for j in range(sub):
            for c in range(0, D, FC):
                g = d2[k0 + j, c : c + FC, :].astype(f32) * h[c : c + FC, :]
                acc_s[0, c : c + FC, :] += g
                g2_s[c : c + FC, lo + j * N : lo + (j + 1) * N] = g.astype(bf16)
        back = dot(w2[0], g2_s[:, lo : lo + w])
        for j in range(sub):
            same = vs[k0 + j, 1:2, :]
            for c in range(0, D, FC):
                g = d1[k0 + j, c : c + FC, :].astype(f32) * back[c : c + FC, j * N : (j + 1) * N]
                gzso[c : c + FC, :] += g
                acc_s[1, c : c + FC, :] += g * same
                g1_s[c : c + FC, lo + j * N : lo + (j + 1) * N] = g.astype(bf16)
        back = dot(wedge[...], g1_s[:, lo : lo + w]) + dot(vsq[0], wide(gy1, k0, sub))
        for j in range(sub):
            ego[0, k0 + j] = up[0, k0 + j].astype(f32) + back[:, j * N : (j + 1) * N]
    g1 = g1_s[...]
    part = dot_t(oh_s[...], g1)

    @pl.when(step == 0)
    def _():
        so[...] = part

    @pl.when(step > 0)
    def _():
        so[...] += part

    dw2o[...] += dot_t(wide(p1, 0, KB), g2_s[...])
    dweo[...] += dot_t(jnp.concatenate([ef[0, j] for j in range(KB)], axis=1), g1)

    @pl.when(step == pl.num_programs(0) - 1)
    def _():
        dbo[0:1, :] += jnp.sum(acc_s[0].T, axis=0, keepdims=True)
        dbo[1:2, :] += jnp.sum(acc_s[1].T, axis=0, keepdims=True)


def msg_bwd(m, S, slot, vs, ef, up, p1, d1, d2, gy1, h, square, wedge, vsq, before, KB=12, sub=6):
    K, N = ef.shape[1], ef.shape[3]
    first = before is None
    extra = [] if first else list(before)
    args = [slot, vs, ef, up, p1, d1, d2, gy1, h, square, wedge, vsq]
    specs = [
        pl.BlockSpec((KB, 2, N), lambda i: (i, 0, 0)),
        pl.BlockSpec((KB, 2, N), lambda i: (i, 0, 0)),
        pl.BlockSpec((1, KB, E, N), lambda i: (m, i, 0, 0)),
        pl.BlockSpec((1, KB, E, N), lambda i: (m, i, 0, 0)),
        pl.BlockSpec((KB, D, N), lambda i: (i, 0, 0)),
        pl.BlockSpec((KB, D, N), lambda i: (i, 0, 0)),
        pl.BlockSpec((KB, D, N), lambda i: (i, 0, 0)),
        pl.BlockSpec((KB, E, N), lambda i: (i, 0, 0)),
        whole(D, N),
        picked(2, D, D),
        whole(E, D),
        picked(0, E, E),
    ]
    aliases = {}
    if not first:
        specs += [whole(D, D), whole(E, D), whole(8, D), pl.BlockSpec(memory_space=pl.ANY)]
        aliases = {len(args) + 3: 0}
    L = KB * N
    return pl.pallas_call(
        functools.partial(msg_bwd_body, m, KB, sub, S, first),
        grid=(K // KB,),
        in_specs=specs,
        out_specs=[
            pl.BlockSpec((1, KB, E, N), lambda i: (m, i, 0, 0)),
            whole(D, N),
            whole(S, D),
            whole(D, D),
            whole(E, D),
            whole(8, D),
        ],
        out_shape=[
            jax.ShapeDtypeStruct(ef.shape, f32),
            jax.ShapeDtypeStruct((D, N), f32),
            jax.ShapeDtypeStruct((S, D), f32),
            jax.ShapeDtypeStruct((D, D), f32),
            jax.ShapeDtypeStruct((E, D), f32),
            jax.ShapeDtypeStruct((8, D), f32),
        ],
        scratch_shapes=[
            pltpu.VMEM((S, L), bf16),
            pltpu.VMEM((D, L), bf16),
            pltpu.VMEM((D, L), bf16),
            pltpu.VMEM((2, D, N), f32),
        ],
        input_output_aliases=aliases,
        compiler_params=pltpu.CompilerParams(vmem_limit_bytes=VMEM_LIMIT),
        name="msg_bwd",
        cost_estimate=pl.CostEstimate(
            flops=2 * N * K * 16 * 65536, bytes_accessed=N * K * D * 10, transcendentals=0
        ),
    )(*args, *extra)


def picked_rows(srow, N, S):
    hit = lax.broadcasted_iota(jnp.int32, (N, S), 0) == srow
    return jnp.where(hit, 1.0, 0.0).astype(bf16)


def split_dot(v, w):
    hi, lo = split2(v)
    return dot(hi, w) + dot(lo, w)


def split_dot_t(v, w):
    hi, lo = split2(v)
    return dot_t(hi, w) + dot_t(lo, w)


def split_tdot(w, v):
    hi, lo = split2(v)
    return tdot(w, hi) + tdot(w, lo)


def scaled(v, row, shift):
    xhat, rs = normed(v)
    return xhat * row + shift, xhat, rs


def node_in_body(x, rows, srow, tags, u1o, sendo):
    _, N, _ = x.shape
    S = srow.shape[2]
    for m in range(x.shape[0]):
        u1 = scaled(x[m].astype(f32), rows[0:1, :], rows[1:2, :])[0].astype(bf16)
        u1o[m] = u1
        oh = picked_rows(srow[m], N, S)
        sendo[m, :, 0:D] = tdot(oh, u1).astype(bf16)
        sendo[m, :, D:] = tdot(oh, tags[m]).astype(bf16)


def node_in(x, rows, srow, tags):
    MB, N, _ = x.shape
    S = srow.shape[2]
    return pl.pallas_call(
        node_in_body,
        out_shape=[
            jax.ShapeDtypeStruct((MB, N, D), bf16),
            jax.ShapeDtypeStruct((MB, S, D + 128), bf16),
        ],
        compiler_params=pltpu.CompilerParams(vmem_limit_bytes=VMEM_LIMIT),
        name="node_in",
    )(x, rows, srow, tags)


def node_mid_body(
    ps, cnt, x, w3, wup, wdown, vin, rows, c4, rowe, srow,
    outo, x1o, a2o, qo, qdo, wo, yso, sendo,
):
    N = x.shape[1]
    S = srow.shape[2]
    cnt_col = cnt[...].T[:, 0:1]
    total = split_dot(ps[...].T, w3[0]) + cnt_col * rows[9:10, :]
    x1 = x[0].astype(f32) + total / jnp.maximum(cnt_col, 1.0)
    x1o[...] = x1
    a2 = scaled(x1, rows[2:3, :], rows[3:4, :])[0].astype(bf16)
    a2o[...] = a2
    out = x1 + rows[10:11, :]
    for c in range(0, F, 512):
        q, qd = gelu_pair(dot(a2, wup[:, c : c + 512]) + c4[0:1, c : c + 512])
        q = q.astype(bf16)
        qo[:, c : c + 512] = q
        qdo[:, c : c + 512] = qd
        out = out + dot(q, wdown[c : c + 512, :])
    outo[...] = out
    w = scaled(out, rows[4:5, :], rows[5:6, :])[0].astype(bf16)
    wo[...] = w
    yso[...] = (dot(w, vin[0]) + rowe[0:1, :]).T
    near = dot(w, vin[1]).astype(bf16)
    sendo[...] = tdot(picked_rows(srow[0], N, S), near).astype(bf16)


def node_mid(m, ps, cnt, x, square, wup, wdown, vin, rows, c4, rowe, srow):
    N = x.shape[1]
    S = srow.shape[2]
    shapes = [
        jax.ShapeDtypeStruct((N, D), f32),
        jax.ShapeDtypeStruct((N, D), f32),
        jax.ShapeDtypeStruct((N, D), bf16),
        jax.ShapeDtypeStruct((N, F), bf16),
        jax.ShapeDtypeStruct((N, F), f32),
        jax.ShapeDtypeStruct((N, D), bf16),
        jax.ShapeDtypeStruct((E, N), f32),
        jax.ShapeDtypeStruct((S, E), bf16),
    ]
    return pl.pallas_call(
        node_mid_body,
        grid=(1,),
        in_specs=[
            whole(D, N), whole(8, N), picked(m, N, D), picked(3, D, D), whole(D, F), whole(F, D),
            whole(2, D, E), whole(16, D), whole(8, F), whole(8, E), picked(m, 1, S),
        ],
        out_specs=[whole(*s.shape) for s in shapes],
        out_shape=shapes,
        compiler_params=pltpu.CompilerParams(vmem_limit_bytes=VMEM_LIMIT),
        name="node_mid",
        cost_estimate=pl.CostEstimate(flops=2 * N * D * F * 2, bytes_accessed=8 << 20, transcendentals=0),
    )(ps, cnt, x, square, wup, wdown, vin, rows, c4, rowe, srow)


def node_back_body(
    inc, srow, gys_t, vin, w, out, x1, a2, q, qd, up, wup, wdown, w3, rows, ps, cnt, *refs
):
    first = len(refs) == 8
    old, (ho, gx1o, dw3o, dupo, ddowno, dvino, vro, vwo) = refs[:-8], refs[-8:]
    N = w.shape[0]
    S = srow.shape[2]

    def put(i, ref, sl, v):
        ref[sl] = v if first else old[i][sl] + v

    picks = picked_rows(srow[0], N, S)
    near = dot(picks, inc[...])
    gys = gys_t[...].T
    wv = w[...]
    put(3, dvino, 0, split_tdot(wv, gys))
    put(3, dvino, 1, split_tdot(wv, near))
    gw = split_dot_t(gys, vin[0]) + split_dot_t(near, vin[1])
    xhat, rs = normed(out[...])
    gx, dg3, db3 = norm_back(xhat, rs, rows[4:5, :], gw)
    gx2 = up[0].astype(f32) + gx
    gy = gx2.astype(bf16)
    dc5 = jnp.sum(gy.astype(f32), axis=0, keepdims=True)
    ga2 = jnp.zeros((N, D), f32)
    for c in range(0, F, 512):
        sl = slice(c, c + 512)
        put(2, ddowno, (sl, slice(None)), tdot(q[:, sl], gy))
        gf = (qd[:, sl] * dot_t(gy, wdown[sl, :])).astype(bf16)
        put(1, dupo, (slice(None), sl), tdot(a2[...], gf))
        put(5, vwo, (slice(0, 1), sl), jnp.sum(gf.astype(f32), axis=0, keepdims=True))
        ga2 = ga2 + dot_t(gf, wup[:, sl])
    xhat, rs = normed(x1[...])
    gx, dg2, db2 = norm_back(xhat, rs, rows[2:3, :], ga2)
    gx1 = gx2 + gx
    gx1o[...] = gx1
    cnt_col = cnt[...].T[:, 0:1]
    g = (gx1 / jnp.maximum(cnt_col, 1.0)).astype(bf16)
    ho[...] = dot_t(g, w3[0]).T
    put(0, dw3o, slice(None), split_dot(ps[...], g))
    dc3 = jnp.sum(g.astype(f32) * cnt_col, axis=0, keepdims=True)
    dd1 = jnp.sum(gys, axis=0, keepdims=True)
    zero = jnp.zeros((1, D - E), f32)
    for i, v in enumerate((dg2, db2, dg3, db3, dc3, dc5, jnp.concatenate([dd1, zero], axis=1))):
        put(4, vro, (slice(i, i + 1), slice(None)), v)
    vro[7:8, :] = jnp.zeros((1, D), f32)
    vwo[1:8, :] = jnp.zeros((7, F), f32)


def node_back(m, inc, srow, gys_t, vin, kept, up, wup, wdown, square, rows, ps, cnt, before):
    out, x1, a2, q, qd, w = kept
    N = w.shape[0]
    S = srow.shape[2]
    shapes = [
        jax.ShapeDtypeStruct((D, N), f32),
        jax.ShapeDtypeStruct((N, D), f32),
        jax.ShapeDtypeStruct((D, D), f32),
        jax.ShapeDtypeStruct((D, F), f32),
        jax.ShapeDtypeStruct((F, D), f32),
        jax.ShapeDtypeStruct((2, D, E), f32),
        jax.ShapeDtypeStruct((8, D), f32),
        jax.ShapeDtypeStruct((8, F), f32),
    ]
    extra = [] if before is None else list(before)
    args = [inc, srow, gys_t, vin, w, out, x1, a2, q, qd, up, wup, wdown, square, rows, ps, cnt]
    aliases = {len(args) + i: 2 + i for i in range(len(extra))}
    return pl.pallas_call(
        node_back_body,
        grid=(1,),
        in_specs=[
            whole(S, E), picked(m, 1, S), whole(E, N), whole(2, D, E), whole(N, D), whole(N, D),
            whole(N, D), whole(N, D), whole(N, F), whole(N, F), picked(m, N, D), whole(D, F),
            whole(F, D), picked(3, D, D), whole(16, D), whole(D, N), whole(8, N),
        ]
        + [whole(*v.shape) for v in extra],
        out_specs=[whole(*s.shape) for s in shapes],
        out_shape=shapes,
        input_output_aliases=aliases,
        compiler_params=pltpu.CompilerParams(vmem_limit_bytes=VMEM_LIMIT),
        name="node_back",
        cost_estimate=pl.CostEstimate(flops=2 * N * D * F * 4, bytes_accessed=20 << 20, transcendentals=0),
    )(*args, *extra)


def node_end_body(inc, srow, gzs_t, u1, x, gx1, wself, wnbr, rows, *refs):
    first = len(refs) == 3
    old, (go, dwo, vro) = refs[:-3], refs[-3:]
    N = u1.shape[1]
    S = srow.shape[2]

    def put(i, ref, sl, v):
        ref[sl] = v if first else old[i][sl] + v

    near = dot(picked_rows(srow[0], N, S), inc[...])
    gzs = gzs_t[...].T
    put(0, dwo, 0, split_tdot(u1[0], gzs))
    put(0, dwo, 1, split_tdot(u1[0], near))
    gu1 = split_dot_t(gzs, wself[0]) + split_dot_t(near, wnbr[0])
    xhat, rs = normed(x[0].astype(f32))
    gx, dg1, db1 = norm_back(xhat, rs, rows[0:1, :], gu1)
    go[...] = gx1[...] + gx
    for i, v in enumerate((dg1, db1, jnp.sum(gzs, axis=0, keepdims=True))):
        put(1, vro, (slice(i, i + 1), slice(None)), v)
    vro[3:8, :] = jnp.zeros((5, D), f32)


def node_end(m, inc, srow, gzs_t, u1, x, gx1, square, rows, before):
    N = x.shape[1]
    S = srow.shape[2]
    shapes = [
        jax.ShapeDtypeStruct((N, D), f32),
        jax.ShapeDtypeStruct((2, D, D), f32),
        jax.ShapeDtypeStruct((8, D), f32),
    ]
    extra = [] if before is None else list(before)
    args = [inc, srow, gzs_t, u1, x, gx1, square, square, rows]
    return pl.pallas_call(
        node_end_body,
        grid=(1,),
        in_specs=[
            whole(S, D), picked(m, 1, S), whole(D, N), picked(m, N, D), picked(m, N, D),
            whole(N, D), picked(0, D, D), picked(1, D, D), whole(16, D),
        ]
        + [whole(*v.shape) for v in extra],
        out_specs=[whole(*s.shape) for s in shapes],
        out_shape=shapes,
        input_output_aliases={len(args) + i: 1 + i for i in range(len(extra))},
        compiler_params=pltpu.CompilerParams(vmem_limit_bytes=VMEM_LIMIT),
        name="node_end",
    )(*args, *extra)


def exchange(rows):
    return lax.all_to_all(rows, ("res", "tp"), split_axis=0, concat_axis=0, tiled=True)


def shards(
    node_feats, edge_feats, slot_index, send_rows, res_mask, chain_ids, node_upstream, edge_upstream,
    *state,
):
    masters, firsts, seconds = state[0:7], state[7:14], state[14:21]
    MB, N, K, _ = edge_feats.shape
    devs = send_rows.shape[2]
    S = devs * send_rows.shape[3]
    low = [v.astype(bf16) for v in masters]
    vec = lax.all_gather(low[6], "tp", axis=0, tiled=True)
    square = lax.all_gather(low[0], "tp", axis=1, tiled=True)
    wedge = lax.all_gather(low[1], "tp", axis=0, tiled=True)
    wup = lax.all_gather(low[2], "tp", axis=0, tiled=True)
    wdown = lax.all_gather(low[3], "tp", axis=0, tiled=True)
    vin = lax.all_gather(low[4], "tp", axis=1, tiled=True)
    vsq = lax.all_gather(low[5], "tp", axis=1, tiled=True)
    vec = vec.astype(f32)
    rows = jnp.pad(vec[: 11 * D].reshape(11, D), ((0, 5), (0, 0)))
    c4 = jnp.pad(vec[11 * D : 11 * D + F].reshape(1, F), ((0, 7), (0, 0)))
    rowe = jnp.pad(vec[11 * D + F :].reshape(3, E), ((0, 5), (0, 0)))

    ef = jnp.transpose(edge_feats, (0, 2, 3, 1))
    eup = jnp.transpose(edge_upstream, (0, 2, 3, 1))
    slot = jnp.transpose(slot_index, (2, 0, 1))
    srow = send_rows.reshape(MB, 1, S)
    own = (res_mask * (chain_ids + 1)).astype(f32)
    tags = jnp.broadcast_to(own.astype(bf16)[:, :, None], (MB, N, 128))

    u1, send = node_in(node_feats, rows, srow, tags)
    tabs = [exchange(send[m])[None] for m in range(MB)]

    mids, fwd, kept = [], [], []
    for m in range(MB):
        a = msg_fwd(0 if False else m, slot, own, ef, tabs[m], u1, square, wedge, rows)
        p1, d1, d2, ps, cnt, vs = a
        fwd.append(a)
        out, x1, a2, q, qd, w, ys, wsend = node_mid(
            m, ps, cnt, node_feats, square, wup, wdown, vin, rows, c4, rowe, srow
        )
        kept.append((out, x1, a2, q, qd, w))
        mids.append((ys, exchange(wsend)))
    before = None
    edges = []
    for m in range(MB):
        ys, tab = mids[m]
        eo, gy1, gys_t, sums, dv, db = edge_net(
            m, slot, fwd[m][5], ef, eup, tab, ys, vsq, rowe, before
        )
        before = (dv, db, eo)
        edges.append((gy1, gys_t, exchange(sums.astype(bf16))))
    dvsq, dbe, edge_out = before
    before = None
    backs = []
    for m in range(MB):
        gy1, gys_t, inc = edges[m]
        p1, d1, d2, ps, cnt, vs = fwd[m]
        ho, gx1, *before = node_back(
            m, inc, srow, gys_t, vin, kept[m], node_upstream, wup, wdown, square, rows, ps, cnt, before
        )
        backs.append((ho, gx1))
    dw3, dup, ddown, dvin, vr2, vw = before
    before = None
    last = []
    for m in range(MB):
        p1, d1, d2, ps, cnt, vs = fwd[m]
        ego, gzs_t, sums, dw2, dwe, dbm = msg_bwd(
            m, S, slot, vs, ef, eup, p1, d1, d2, edges[m][0], backs[m][0], square, wedge, vsq, before
        )
        before = (dw2, dwe, dbm, ego)
        last.append((gzs_t, exchange(sums.astype(bf16))))
    dw2, dwe, dbm, edge_grad = before
    before = None
    node_grads = []
    for m in range(MB):
        gzs_t, inc = last[m]
        ng, *before = node_end(m, inc, srow, gzs_t, u1, node_feats, backs[m][1], square, rows, before)
        node_grads.append(ng)
    dws, vr1 = before
    vec_grad = jnp.concatenate(
        [
            vr1[0], vr1[1], vr2[0], vr2[1], vr2[2], vr2[3], vr1[2], dbm[1], dbm[0], vr2[4], vr2[5],
            vw[0], vr2[6, :E], dbe[1], dbe[2],
        ]
    )
    locals_ = (
        jnp.stack([dws[0], dws[1], dw2, dw3]), dwe, dup, ddown, dvin, dvsq, vec_grad,
    )
    dims = (1, 0, 0, 0, 1, 1, 0)
    total = lax.psum(
        tuple(
            lax.psum_scatter(g, "tp", scatter_dimension=d, tiled=True) for g, d in zip(locals_, dims)
        ),
        "res",
    )
    square_sum = jnp.zeros((), f32)
    for part in total:
        square_sum = square_sum + jnp.sum(part * part)
    grad_norm = jnp.sqrt(lax.psum(square_sum, "tp"))
    scale = clip_norm / jnp.maximum(grad_norm, clip_norm)
    first_fix = 1.0 - beta_first**STEP
    second_fix = 1.0 - beta_second**STEP
    new_w, new_f, new_s = [], [], []
    for i in range(7):
        decay, rate = (decay_rate, learn_rate) if i < 6 else (0.0, vector_rate)
        clipped = total[i] * scale
        nf = beta_first * firsts[i] + (1.0 - beta_first) * clipped
        ns = beta_second * seconds[i] + (1.0 - beta_second) * clipped * clipped
        step = nf / first_fix / (jnp.sqrt(ns / second_fix) + adam_eps)
        new_w.append(masters[i] - rate * (step + decay * masters[i]))
        new_f.append(nf)
        new_s.append(ns)
    return (
        jnp.stack([k[0] for k in kept]),
        jnp.transpose(edge_out, (0, 3, 1, 2)),
        jnp.stack(node_grads),
        jnp.transpose(edge_grad, (0, 3, 1, 2)),
        grad_norm.reshape(1),
        *new_w,
        *new_f,
        *new_s,
    )


def solution(mesh):
    lead = ("res", "tp")
    feats = (
        P(None, lead, None),
        P(None, lead, None, None),
        P(None, lead, None),
        P(None, lead, None, None),
        P(None, lead),
        P(None, lead),
        P(None, lead, None),
        P(None, lead, None, None),
    )
    params = (
        P(None, "tp", None),
        P("tp", None),
        P("tp", None),
        P("tp", None),
        P(None, "tp", None),
        P(None, "tp", None),
        P("tp"),
    )
    node, edge = P(None, lead, None), P(None, lead, None, None)
    return jax.shard_map(
        shards,
        mesh=mesh,
        in_specs=feats + params * 3,
        out_specs=(node, edge, node, edge, P()) + params * 3,
        check_vma=False,
    )
```

```python
import functools

import jax
import jax.numpy as jnp
from jax import lax
from jax.experimental import pallas as pl
from jax.experimental.pallas import tpu as pltpu
from jax.sharding import PartitionSpec as P

D = 512
E = 192
F = 2048
STEP = 5

norm_eps = 1e-05
learn_rate = 0.03
vector_rate = 0.25
beta_first = 0.5
beta_second = 0.5
adam_eps = 1e-08
decay_rate = 0.01
clip_norm = 1.0

C0 = 0.7978845608028654
C1 = C0 * 0.044715
bf16 = jnp.bfloat16
f32 = jnp.float32
VMEM_LIMIT = 58 * 1024 * 1024


def gelu_pair(z):
    q = z * z
    t = jnp.tanh(z * (q * C1 + C0))
    s = 0.5 * t + 0.5
    p = z * s
    d = s + (p - p * s) * (q * (6.0 * C1) + 2.0 * C0)
    return p, d


def dot(a, b):
    return jnp.dot(a, b, preferred_element_type=f32)


def dot_t(a, b):
    return lax.dot_general(a, b, (((1,), (1,)), ((), ())), preferred_element_type=f32)


def tdot(a, b):
    return lax.dot_general(a, b, (((0,), (0,)), ((), ())), preferred_element_type=f32)


def turned(v):
    n = v.shape[1]
    eye = lax.broadcasted_iota(jnp.int32, (n, n), 0) == lax.broadcasted_iota(jnp.int32, (n, n), 1)
    return dot_t(jnp.where(eye, 1.0, 0.0).astype(bf16), v)


def split2(v):
    hi = v.astype(bf16)
    lo = (v - hi.astype(f32)).astype(bf16)
    return hi, lo


def normed(v):
    centred = v - jnp.mean(v, axis=-1, keepdims=True)
    spread = jnp.mean(centred * centred, axis=-1, keepdims=True)
    rs = lax.rsqrt(spread + norm_eps)
    return centred * rs, rs


def norm_back(xhat, rs, gain, grad):
    gn = grad * gain
    gx = rs * (
        gn
        - jnp.mean(gn, axis=-1, keepdims=True)
        - xhat * jnp.mean(gn * xhat, axis=-1, keepdims=True)
    )
    return gx, jnp.sum(grad * xhat, axis=0, keepdims=True), jnp.sum(grad, axis=0, keepdims=True)


def whole(*dims):
    zero = (0,) * len(dims)
    return pl.BlockSpec(dims, lambda i: zero)


def picked(m, *dims):
    index = (m,) + (0,) * len(dims)
    return pl.BlockSpec((1,) + dims, lambda i: index)


def one_hots(slot, m, k0, count, S):
    n = slot.shape[2]
    iota = lax.broadcasted_iota(jnp.int32, (S, n), 0)
    return jnp.concatenate(
        [
            jnp.where(iota == slot[k0 + j, m : m + 1, :], 1.0, 0.0).astype(bf16)
            for j in range(count)
        ],
        axis=1,
    )


def wide(ref3, k0, count):
    return jnp.concatenate([ref3[k0 + j] for j in range(count)], axis=1)


def stacked(ref, lo=0, n=None, c0=0, cols=D):
    n = ref.shape[1] if n is None else n
    if n % 16 == 0:
        return ref[:, lo : lo + n, c0 : c0 + cols].reshape(ref.shape[0] * n, cols)
    parts = [ref[t, :, c0 : c0 + cols].astype(f32)[lo : lo + n] for t in range(ref.shape[0])]
    return jnp.concatenate(parts, axis=0).astype(bf16)


def unit(T, n, index):
    return pl.BlockSpec((T, n, D), lambda i: (0, index, 0))


def msg_fwd_body(
    m, KB, sub, S, slot, own, ef, tab, x, wnbr, wself, wedge, w2, rows,
    p1o, d1o, d2o, pso, cnto, vso, tt_s, zs_s, zc_s, we_s, w2_s, c2_s,
):
    step = pl.program_id(0)
    N = ef.shape[3]

    @pl.when(step == 0)
    def _():
        g1, b1 = rows[0:1, :], rows[1:2, :]
        wn = stacked(wnbr)
        for c in range(0, S, 512):
            near = (normed(tab[c : c + 512, 0:D].astype(f32))[0] * g1 + b1).astype(bf16)
            tt_s[0:D, c : c + 512] = dot(near, wn).T.astype(bf16)
            tags = tab[c : c + 512, D : D + 128].astype(f32).T
            tt_s[D:, c : c + 512] = tags[0:16, :].astype(bf16)
        u1 = (normed(x[0].astype(f32))[0] * g1 + b1).astype(bf16)
        zs = dot(u1, stacked(wself)) + rows[6:7, :]
        zs_s[...] = zs.T
        zc_s[...] = (zs + rows[7:8, :]).T
        we_s[...] = stacked(wedge, 0, E // wedge.shape[0]).astype(f32).T.astype(bf16)
        w2_s[...] = stacked(w2).astype(f32).T.astype(bf16)
        c2_s[...] = jnp.broadcast_to(rows[8:9, :], (N, D)).T
        pso[...] = jnp.zeros_like(pso)
        cnto[...] = jnp.zeros_like(cnto)

    own_row = own[m : m + 1, :]
    FC = 128
    for s in range(KB // sub):
        k0 = s * sub
        oht = one_hots(slot, m, k0, sub, S)
        z1 = dot(tt_s[...], oht)
        ze = dot(we_s[...], jnp.concatenate([ef[0, k0 + j] for j in range(sub)], axis=1))
        vals = []
        parts = []
        for j in range(sub):
            k = k0 + j
            lo, hi = j * N, (j + 1) * N
            tag = z1[D : D + 1, lo:hi]
            v = jnp.where((tag > 0.0) & (own_row > 0.0), 1.0, 0.0)
            same = tag == own_row
            vals.append(v)
            vso[k, 0:1, :] = v
            vso[k, 1:2, :] = jnp.where(same, 1.0, 0.0)
            cnto[0:1, :] += v
            for c in range(0, D, FC):
                base = jnp.where(same, zc_s[c : c + FC, :], zs_s[c : c + FC, :])
                p, d = gelu_pair(z1[c : c + FC, lo:hi] + ze[c : c + FC, lo:hi] + base)
                p1o[k, c : c + FC, :] = p.astype(bf16)
                d1o[k, c : c + FC, :] = d.astype(bf16)
        z2 = dot(w2_s[...], wide(p1o, k0, sub))
        for j in range(sub):
            k = k0 + j
            lo, hi = j * N, (j + 1) * N
            for c in range(0, D, FC):
                p, d = gelu_pair(z2[c : c + FC, lo:hi] + c2_s[c : c + FC, :])
                d2o[k, c : c + FC, :] = (d * vals[j]).astype(bf16)
                pso[c : c + FC, :] += p * vals[j]


def msg_fwd(m, slot, own, ef, tab, x, l0, l1, rows, KB=12, sub=6):
    K, N = ef.shape[1], ef.shape[3]
    S = tab.shape[0]
    T = l0.shape[0]
    U = D // T
    return pl.pallas_call(
        functools.partial(msg_fwd_body, m, KB, sub, S),
        grid=(K // KB,),
        in_specs=[
            pl.BlockSpec((KB, 2, N), lambda i: (i, 0, 0)),
            whole(2, N),
            pl.BlockSpec((1, KB, E, N), lambda i: (m, i, 0, 0)),
            whole(S, D + 128),
            picked(m, N, D),
            unit(T, U, 1),
            unit(T, U, 0),
            unit(T, U // 2, 2),
            unit(T, U, 0),
            whole(16, D),
        ],
        out_specs=[
            pl.BlockSpec((KB, D, N), lambda i: (i, 0, 0)),
            pl.BlockSpec((KB, D, N), lambda i: (i, 0, 0)),
            pl.BlockSpec((KB, D, N), lambda i: (i, 0, 0)),
            whole(D, N),
            whole(8, N),
            pl.BlockSpec((KB, 2, N), lambda i: (i, 0, 0)),
        ],
        out_shape=[
            jax.ShapeDtypeStruct((K, D, N), bf16),
            jax.ShapeDtypeStruct((K, D, N), bf16),
            jax.ShapeDtypeStruct((K, D, N), bf16),
            jax.ShapeDtypeStruct((D, N), f32),
            jax.ShapeDtypeStruct((8, N), f32),
            jax.ShapeDtypeStruct((K, 2, N), f32),
        ],
        scratch_shapes=[
            pltpu.VMEM((D + 16, S), bf16),
            pltpu.VMEM((D, N), f32),
            pltpu.VMEM((D, N), f32),
            pltpu.VMEM((D, E), bf16),
            pltpu.VMEM((D, D), bf16),
            pltpu.VMEM((D, N), f32),
        ],
        compiler_params=pltpu.CompilerParams(vmem_limit_bytes=VMEM_LIMIT),
        name="msg_fwd",
        cost_estimate=pl.CostEstimate(
            flops=2 * N * K * 10 * 65536, bytes_accessed=N * K * D * 6, transcendentals=0
        ),
    )(slot, own, ef, tab, x, l0, l0, l1, l1, rows)


def edge_body(m, KB, sub, S, first, slot, vs, ef, up, tab, ys, strips, rows, *refs):
    refs, scr = refs[:-11], refs[-11:]
    (eo, gy1o, gyso, so, dvo, dbo) = refs[-6:]
    (nt_s, vsq, vt_s, b_s, oh_s, r1_s, r2_s, g3_s, g2_s, ef_s, acc_s) = scr
    step = pl.program_id(0)
    N = ef.shape[3]

    @pl.when(step == 0)
    def _():
        nt_s[...] = turned(tab[...]).astype(bf16)
        EP, SP = E // strips.shape[0], strips.shape[1] // 2
        for i, (lo, c0) in enumerate(((0, 0), (0, 256), (SP, 0))):
            vsq[i] = stacked(strips, lo, EP, c0, E)
            vt_s[i] = turned(vsq[i]).astype(bf16)
        for i in range(2):
            b_s[i] = jnp.broadcast_to(rows[i + 1 : i + 2, :], (N, E)).T
        gyso[...] = jnp.zeros_like(gyso)
        acc_s[...] = jnp.zeros_like(acc_s)
        if first:
            dvo[...] = jnp.zeros_like(dvo)
            dbo[...] = jnp.zeros_like(dbo)
        else:
            dvo[...] = refs[0][...]
            dbo[...] = refs[1][...]

    w = sub * N
    for s in range(KB // sub):
        k0 = s * sub
        lo = s * w
        oht = one_hots(slot, m, k0, sub, S)
        oh_s[:, lo : lo + w] = oht
        eft = jnp.concatenate([ef[0, k0 + j] for j in range(sub)], axis=1)
        ef_s[:, lo : lo + w] = eft
        base = jnp.concatenate([ys[...]] * sub, axis=1)
        r1, e1 = gelu_pair(dot(nt_s[...], oht) + dot(vt_s[0], eft) + base)
        r1 = r1.astype(bf16)
        r1_s[:, lo : lo + w] = r1
        r2, e2 = gelu_pair(dot(vt_s[1], r1) + jnp.concatenate([b_s[0]] * sub, axis=1))
        r2 = r2.astype(bf16)
        r2_s[:, lo : lo + w] = r2
        y3 = dot(vt_s[2], r2)
        for j in range(sub):
            v = vs[k0 + j, 0:1, :]
            eo[0, k0 + j] = ef[0, k0 + j].astype(f32) + v * (y3[:, j * N : (j + 1) * N] + b_s[1])
            g3f = v * up[0, k0 + j].astype(f32)
            acc_s[1] += g3f
            g3_s[:, lo + j * N : lo + (j + 1) * N] = g3f.astype(bf16)
        g2 = (e2 * dot(vsq[2], g3_s[:, lo : lo + w])).astype(bf16)
        g2_s[:, lo : lo + w] = g2
        g1 = (e1 * dot(vsq[1], g2)).astype(bf16)
        for j in range(sub):
            acc_s[0] += g2[:, j * N : (j + 1) * N].astype(f32)
            gyso[...] += g1[:, j * N : (j + 1) * N].astype(f32)
            gy1o[k0 + j] = g1[:, j * N : (j + 1) * N]
    g1 = wide(gy1o, 0, KB)
    part = dot_t(oh_s[...], g1)

    @pl.when(step == 0)
    def _():
        so[...] = part

    @pl.when(step > 0)
    def _():
        so[...] += part

    dvo[2] += dot_t(r2_s[...], g3_s[...])
    dvo[1] += dot_t(r1_s[...], g2_s[...])
    dvo[0] += dot_t(ef_s[...], g1)

    @pl.when(step == pl.num_programs(0) - 1)
    def _():
        dbo[1:2, :] += jnp.sum(acc_s[0].T, axis=0, keepdims=True)
        dbo[2:3, :] += jnp.sum(acc_s[1].T, axis=0, keepdims=True)


def edge_net(m, slot, vs, ef, up, tab, ys, m1, rows, before, KB=12, sub=6):
    K, N = ef.shape[1], ef.shape[3]
    S = tab.shape[0]
    first = before is None
    extra = [] if first else list(before)
    args = [slot, vs, ef, up, tab, ys, m1, rows]
    T = m1.shape[0]
    specs = [
        pl.BlockSpec((KB, 2, N), lambda i: (i, 0, 0)),
        pl.BlockSpec((KB, 2, N), lambda i: (i, 0, 0)),
        pl.BlockSpec((1, KB, E, N), lambda i: (m, i, 0, 0)),
        pl.BlockSpec((1, KB, E, N), lambda i: (m, i, 0, 0)),
        whole(S, E),
        whole(E, N),
        unit(T, D // T, 5),
        whole(8, E),
    ]
    aliases = {}
    if not first:
        specs += [whole(3, E, E), whole(8, E), pl.BlockSpec(memory_space=pl.ANY)]
        aliases = {len(args) + 2: 0}
    L = KB * N
    return pl.pallas_call(
        functools.partial(edge_body, m, KB, sub, S, first),
        grid=(K // KB,),
        in_specs=specs,
        out_specs=[
            pl.BlockSpec((1, KB, E, N), lambda i: (m, i, 0, 0)),
            pl.BlockSpec((KB, E, N), lambda i: (i, 0, 0)),
            whole(E, N),
            whole(S, E),
            whole(3, E, E),
            whole(8, E),
        ],
        out_shape=[
            jax.ShapeDtypeStruct(ef.shape, f32),
            jax.ShapeDtypeStruct((K, E, N), bf16),
            jax.ShapeDtypeStruct((E, N), f32),
            jax.ShapeDtypeStruct((S, E), f32),
            jax.ShapeDtypeStruct((3, E, E), f32),
            jax.ShapeDtypeStruct((8, E), f32),
        ],
        scratch_shapes=[
            pltpu.VMEM((E, S), bf16),
            pltpu.VMEM((3, E, E), bf16),
            pltpu.VMEM((3, E, E), bf16),
            pltpu.VMEM((2, E, N), f32),
            pltpu.VMEM((S, L), bf16),
            pltpu.VMEM((E, L), bf16),
            pltpu.VMEM((E, L), bf16),
            pltpu.VMEM((E, L), bf16),
            pltpu.VMEM((E, L), bf16),
            pltpu.VMEM((E, L), bf16),
            pltpu.VMEM((2, E, N), f32),
        ],
        input_output_aliases=aliases,
        compiler_params=pltpu.CompilerParams(vmem_limit_bytes=VMEM_LIMIT),
        name="edge_net",
        cost_estimate=pl.CostEstimate(
            flops=2 * N * K * 12 * 65536, bytes_accessed=N * K * E * 12, transcendentals=0
        ),
    )(*args, *extra)


def msg_bwd_body(
    m, KB, sub, S, first, slot, vs, ef, up, p1, d1, d2, gy1, h, w2u, strip, strips, *refs
):
    refs, scr = refs[:-7], refs[-7:]
    (ego, gzso, so, dw2o, dweo, dbo) = refs[-6:]
    (oh_s, g2_s, g1_s, acc_s, w2, wedge, ve) = scr
    step = pl.program_id(0)
    N = ef.shape[3]

    @pl.when(step == 0)
    def _():
        w2[...] = stacked(w2u)
        wedge[...] = stacked(strip, 0, E // strip.shape[0])
        ve[...] = stacked(strips, 0, E // strip.shape[0], 0, E)
        gzso[...] = jnp.zeros_like(gzso)
        acc_s[...] = jnp.zeros_like(acc_s)
        if first:
            dw2o[...] = jnp.zeros_like(dw2o)
            dweo[...] = jnp.zeros_like(dweo)
            dbo[...] = jnp.zeros_like(dbo)
        else:
            dw2o[...] = refs[0][...]
            dweo[...] = refs[1][...]
            dbo[...] = refs[2][...]

    w = sub * N
    FC = 128
    for s in range(KB // sub):
        k0 = s * sub
        lo = s * w
        oh_s[:, lo : lo + w] = one_hots(slot, m, k0, sub, S)
        for j in range(sub):
            for c in range(0, D, FC):
                g = d2[k0 + j, c : c + FC, :].astype(f32) * h[c : c + FC, :]
                acc_s[0, c : c + FC, :] += g
                g2_s[c : c + FC, lo + j * N : lo + (j + 1) * N] = g.astype(bf16)
        back = dot(w2[...], g2_s[:, lo : lo + w])
        for j in range(sub):
            same = vs[k0 + j, 1:2, :]
            for c in range(0, D, FC):
                g = d1[k0 + j, c : c + FC, :].astype(f32) * back[c : c + FC, j * N : (j + 1) * N]
                gzso[c : c + FC, :] += g
                acc_s[1, c : c + FC, :] += g * same
                g1_s[c : c + FC, lo + j * N : lo + (j + 1) * N] = g.astype(bf16)
        back = dot(wedge[...], g1_s[:, lo : lo + w]) + dot(ve[...], wide(gy1, k0, sub))
        for j in range(sub):
            ego[0, k0 + j] = up[0, k0 + j].astype(f32) + back[:, j * N : (j + 1) * N]
    g1 = g1_s[...]
    part = dot_t(oh_s[...], g1)

    @pl.when(step == 0)
    def _():
        so[...] = part

    @pl.when(step > 0)
    def _():
        so[...] += part

    dw2o[...] += dot_t(wide(p1, 0, KB), g2_s[...])
    dweo[...] += dot_t(jnp.concatenate([ef[0, j] for j in range(KB)], axis=1), g1)

    @pl.when(step == pl.num_programs(0) - 1)
    def _():
        dbo[0:1, :] += jnp.sum(acc_s[0].T, axis=0, keepdims=True)
        dbo[1:2, :] += jnp.sum(acc_s[1].T, axis=0, keepdims=True)


def msg_bwd(m, S, slot, vs, ef, up, p1, d1, d2, gy1, h, l1, m1, before, KB=12, sub=6):
    K, N = ef.shape[1], ef.shape[3]
    first = before is None
    extra = [] if first else list(before)
    args = [slot, vs, ef, up, p1, d1, d2, gy1, h, l1, l1, m1]
    T = l1.shape[0]
    U = D // T
    specs = [
        pl.BlockSpec((KB, 2, N), lambda i: (i, 0, 0)),
        pl.BlockSpec((KB, 2, N), lambda i: (i, 0, 0)),
        pl.BlockSpec((1, KB, E, N), lambda i: (m, i, 0, 0)),
        pl.BlockSpec((1, KB, E, N), lambda i: (m, i, 0, 0)),
        pl.BlockSpec((KB, D, N), lambda i: (i, 0, 0)),
        pl.BlockSpec((KB, D, N), lambda i: (i, 0, 0)),
        pl.BlockSpec((KB, D, N), lambda i: (i, 0, 0)),
        pl.BlockSpec((KB, E, N), lambda i: (i, 0, 0)),
        whole(D, N),
        unit(T, U, 0),
        unit(T, U // 2, 2),
        unit(T, U // 2, 10),
    ]
    aliases = {}
    if not first:
        specs += [whole(D, D), whole(E, D), whole(8, D), pl.BlockSpec(memory_space=pl.ANY)]
        aliases = {len(args) + 3: 0}
    L = KB * N
    return pl.pallas_call(
        functools.partial(msg_bwd_body, m, KB, sub, S, first),
        grid=(K // KB,),
        in_specs=specs,
        out_specs=[
            pl.BlockSpec((1, KB, E, N), lambda i: (m, i, 0, 0)),
            whole(D, N),
            whole(S, D),
            whole(D, D),
            whole(E, D),
            whole(8, D),
        ],
        out_shape=[
            jax.ShapeDtypeStruct(ef.shape, f32),
            jax.ShapeDtypeStruct((D, N), f32),
            jax.ShapeDtypeStruct((S, D), f32),
            jax.ShapeDtypeStruct((D, D), f32),
            jax.ShapeDtypeStruct((E, D), f32),
            jax.ShapeDtypeStruct((8, D), f32),
        ],
        scratch_shapes=[
            pltpu.VMEM((S, L), bf16),
            pltpu.VMEM((D, L), bf16),
            pltpu.VMEM((D, L), bf16),
            pltpu.VMEM((2, D, N), f32),
            pltpu.VMEM((D, D), bf16),
            pltpu.VMEM((E, D), bf16),
            pltpu.VMEM((E, E), bf16),
        ],
        input_output_aliases=aliases,
        compiler_params=pltpu.CompilerParams(vmem_limit_bytes=VMEM_LIMIT),
        name="msg_bwd",
        cost_estimate=pl.CostEstimate(
            flops=2 * N * K * 16 * 65536, bytes_accessed=N * K * D * 10, transcendentals=0
        ),
    )(*args, *extra)


def picked_rows(srow, N, S):
    hit = lax.broadcasted_iota(jnp.int32, (N, S), 0) == srow
    return jnp.where(hit, 1.0, 0.0).astype(bf16)


def split_dot(v, w):
    hi, lo = split2(v)
    return dot(hi, w) + dot(lo, w)


def split_dot_t(v, w):
    hi, lo = split2(v)
    return dot_t(hi, w) + dot_t(lo, w)


def split_tdot(w, v):
    hi, lo = split2(v)
    return tdot(w, hi) + tdot(w, lo)


def scaled(v, row, shift):
    xhat, rs = normed(v)
    return xhat * row + shift, xhat, rs


def node_in_body(x, srow, tags, sendo):
    _, N, _ = x.shape
    S = srow.shape[2]
    for m in range(x.shape[0]):
        oh = picked_rows(srow[m], N, S)
        sendo[m, :, 0:D] = tdot(oh, x[m]).astype(bf16)
        sendo[m, :, D:] = tdot(oh, tags[m]).astype(bf16)


def node_in(x, srow, tags):
    MB, N, _ = x.shape
    S = srow.shape[2]
    return pl.pallas_call(
        node_in_body,
        out_shape=jax.ShapeDtypeStruct((MB, S, D + 128), bf16),
        compiler_params=pltpu.CompilerParams(vmem_limit_bytes=VMEM_LIMIT),
        name="node_in",
    )(x, srow, tags)


def node_mid_body(
    ps, cnt, x, w3, wup, wdown, vinu, rows, c4, rowe, srow,
    outo, x1o, a2o, qo, qdo, wo, yso, sendo,
):
    N = x.shape[1]
    S = srow.shape[2]
    U = vinu.shape[1]
    cnt_col = cnt[...].T[:, 0:1]
    total = split_dot(ps[...].T, stacked(w3)) + cnt_col * rows[9:10, :]
    x1 = x[0].astype(f32) + total / jnp.maximum(cnt_col, 1.0)
    x1o[...] = x1
    a2 = scaled(x1, rows[2:3, :], rows[3:4, :])[0].astype(bf16)
    a2o[...] = a2
    out = x1 + rows[10:11, :]
    wd = stacked(wdown)
    for c in range(0, F, 512):
        q, qd = gelu_pair(dot(a2, stacked(wup, c // 512 * U, U)) + c4[0:1, c : c + 512])
        q = q.astype(bf16)
        qo[:, c : c + 512] = q
        qdo[:, c : c + 512] = qd
        out = out + dot(q, wd[c : c + 512, :])
    outo[...] = out
    w = scaled(out, rows[4:5, :], rows[5:6, :])[0].astype(bf16)
    wo[...] = w
    yso[...] = (dot(w, stacked(vinu, 0, U, 0, E)) + rowe[0:1, :]).T
    near = dot(w, stacked(vinu, 0, U, 256, E)).astype(bf16)
    sendo[...] = tdot(picked_rows(srow[0], N, S), near).astype(bf16)


def node_mid(m, ps, cnt, x, m0, m1, rows, c4, rowe, srow):
    N = x.shape[1]
    S = srow.shape[2]
    T = m0.shape[0]
    U = D // T
    shapes = [
        jax.ShapeDtypeStruct((N, D), f32),
        jax.ShapeDtypeStruct((N, D), f32),
        jax.ShapeDtypeStruct((N, D), bf16),
        jax.ShapeDtypeStruct((N, F), bf16),
        jax.ShapeDtypeStruct((N, F), f32),
        jax.ShapeDtypeStruct((N, D), bf16),
        jax.ShapeDtypeStruct((E, N), f32),
        jax.ShapeDtypeStruct((S, E), bf16),
    ]
    return pl.pallas_call(
        node_mid_body,
        grid=(1,),
        in_specs=[
            whole(D, N), whole(8, N), picked(m, N, D), unit(T, U, 4), unit(T, 4 * U, 0),
            unit(T, 4 * U, 0), unit(T, U, 4), whole(16, D), whole(8, F), whole(8, E), picked(m, 1, S),
        ],
        out_specs=[whole(*s.shape) for s in shapes],
        out_shape=shapes,
        compiler_params=pltpu.CompilerParams(vmem_limit_bytes=VMEM_LIMIT),
        name="node_mid",
        cost_estimate=pl.CostEstimate(flops=2 * N * D * F * 2, bytes_accessed=8 << 20, transcendentals=0),
    )(ps, cnt, x, m0, m1, m0, m1, rows, c4, rowe, srow)


def node_back_body(
    inc, srow, gys_t, vinu, w, out, x1, a2, q, qd, up, wup, wdown, w3, rows, ps, cnt, *refs
):
    first = len(refs) == 8
    old, (ho, gx1o, dw3o, dupo, ddowno, dvino, vro, vwo) = refs[:-8], refs[-8:]
    N = w.shape[0]
    S = srow.shape[2]
    U = vinu.shape[1]
    w3v, wd = stacked(w3), stacked(wdown)

    def put(i, ref, sl, v):
        ref[sl] = v if first else old[i][sl] + v

    picks = picked_rows(srow[0], N, S)
    near = dot(picks, inc[...])
    gys = gys_t[...].T
    wv = w[...]
    put(3, dvino, 0, split_tdot(wv, gys))
    put(3, dvino, 1, split_tdot(wv, near))
    gw = split_dot_t(gys, stacked(vinu, 0, U, 0, E)) + split_dot_t(
        near, stacked(vinu, 0, U, 256, E)
    )
    xhat, rs = normed(out[...])
    gx, dg3, db3 = norm_back(xhat, rs, rows[4:5, :], gw)
    gx2 = up[0].astype(f32) + gx
    gy = gx2.astype(bf16)
    dc5 = jnp.sum(gy.astype(f32), axis=0, keepdims=True)
    ga2 = jnp.zeros((N, D), f32)
    for c in range(0, F, 512):
        sl = slice(c, c + 512)
        put(2, ddowno, (sl, slice(None)), tdot(q[:, sl], gy))
        gf = (qd[:, sl] * dot_t(gy, wd[sl, :])).astype(bf16)
        put(1, dupo, (slice(None), sl), tdot(a2[...], gf))
        put(5, vwo, (slice(0, 1), sl), jnp.sum(gf.astype(f32), axis=0, keepdims=True))
        ga2 = ga2 + dot_t(gf, stacked(wup, c // 512 * U, U))
    xhat, rs = normed(x1[...])
    gx, dg2, db2 = norm_back(xhat, rs, rows[2:3, :], ga2)
    gx1 = gx2 + gx
    gx1o[...] = gx1
    cnt_col = cnt[...].T[:, 0:1]
    g = (gx1 / jnp.maximum(cnt_col, 1.0)).astype(bf16)
    ho[...] = dot_t(g, w3v).T
    put(0, dw3o, slice(None), split_dot(ps[...], g))
    dc3 = jnp.sum(g.astype(f32) * cnt_col, axis=0, keepdims=True)
    dd1 = jnp.sum(gys, axis=0, keepdims=True)
    zero = jnp.zeros((1, D - E), f32)
    for i, v in enumerate((dg2, db2, dg3, db3, dc3, dc5, jnp.concatenate([dd1, zero], axis=1))):
        put(4, vro, (slice(i, i + 1), slice(None)), v)
    vro[7:8, :] = jnp.zeros((1, D), f32)
    vwo[1:8, :] = jnp.zeros((7, F), f32)


def node_back(m, inc, srow, gys_t, kept, up, m0, m1, rows, ps, cnt, before):
    out, x1, a2, q, qd, w = kept
    N = w.shape[0]
    S = srow.shape[2]
    shapes = [
        jax.ShapeDtypeStruct((D, N), f32),
        jax.ShapeDtypeStruct((N, D), f32),
        jax.ShapeDtypeStruct((D, D), f32),
        jax.ShapeDtypeStruct((D, F), f32),
        jax.ShapeDtypeStruct((F, D), f32),
        jax.ShapeDtypeStruct((2, D, E), f32),
        jax.ShapeDtypeStruct((8, D), f32),
        jax.ShapeDtypeStruct((8, F), f32),
    ]
    extra = [] if before is None else list(before)
    args = [inc, srow, gys_t, m1, w, out, x1, a2, q, qd, up, m1, m0, m0, rows, ps, cnt]
    T = m0.shape[0]
    U = D // T
    aliases = {len(args) + i: 2 + i for i in range(len(extra))}
    return pl.pallas_call(
        node_back_body,
        grid=(1,),
        in_specs=[
            whole(S, E), picked(m, 1, S), whole(E, N), unit(T, U, 4), whole(N, D), whole(N, D),
            whole(N, D), whole(N, D), whole(N, F), whole(N, F), picked(m, N, D), unit(T, 4 * U, 0),
            unit(T, 4 * U, 0), unit(T, U, 4), whole(16, D), whole(D, N), whole(8, N),
        ]
        + [whole(*v.shape) for v in extra],
        out_specs=[whole(*s.shape) for s in shapes],
        out_shape=shapes,
        input_output_aliases=aliases,
        compiler_params=pltpu.CompilerParams(vmem_limit_bytes=VMEM_LIMIT),
        name="node_back",
        cost_estimate=pl.CostEstimate(flops=2 * N * D * F * 4, bytes_accessed=20 << 20, transcendentals=0),
    )(*args, *extra)


def node_end_body(inc, srow, gzs_t, x, gx1, wself, wnbr, rows, *refs):
    first = len(refs) == 3
    old, (go, dwo, vro) = refs[:-3], refs[-3:]
    N = x.shape[1]
    S = srow.shape[2]
    xhat, rs = normed(x[0].astype(f32))
    u1 = (xhat * rows[0:1, :] + rows[1:2, :]).astype(bf16)

    def put(i, ref, sl, v):
        ref[sl] = v if first else old[i][sl] + v

    near = dot(picked_rows(srow[0], N, S), inc[...])
    gzs = gzs_t[...].T
    put(0, dwo, 0, split_tdot(u1, gzs))
    put(0, dwo, 1, split_tdot(u1, near))
    gu1 = split_dot_t(gzs, stacked(wself)) + split_dot_t(near, stacked(wnbr))
    gx, dg1, db1 = norm_back(xhat, rs, rows[0:1, :], gu1)
    go[...] = gx1[...] + gx
    for i, v in enumerate((dg1, db1, jnp.sum(gzs, axis=0, keepdims=True))):
        put(1, vro, (slice(i, i + 1), slice(None)), v)
    vro[3:8, :] = jnp.zeros((5, D), f32)


def node_end(m, inc, srow, gzs_t, x, gx1, l0, rows, before):
    T = l0.shape[0]
    U = D // T
    N = x.shape[1]
    S = srow.shape[2]
    shapes = [
        jax.ShapeDtypeStruct((N, D), f32),
        jax.ShapeDtypeStruct((2, D, D), f32),
        jax.ShapeDtypeStruct((8, D), f32),
    ]
    extra = [] if before is None else list(before)
    args = [inc, srow, gzs_t, x, gx1, l0, l0, rows]
    return pl.pallas_call(
        node_end_body,
        grid=(1,),
        in_specs=[
            whole(S, D), picked(m, 1, S), whole(D, N), picked(m, N, D),
            whole(N, D), unit(T, U, 0), unit(T, U, 1), whole(16, D),
        ]
        + [whole(*v.shape) for v in extra],
        out_specs=[whole(*s.shape) for s in shapes],
        out_shape=shapes,
        input_output_aliases={len(args) + i: 1 + i for i in range(len(extra))},
        compiler_params=pltpu.CompilerParams(vmem_limit_bytes=VMEM_LIMIT),
        name="node_end",
    )(*args, *extra)


def place(R, T):
    U = D // T
    lift = lambda rows: -(-rows // (16 * R)) * 16 * R
    sizes = (lift(2 * U), lift(U + U // 2 + 16), lift(5 * U), lift(6 * U))
    return U, U // 2, E // T, sizes


def bit(r, b):
    return (r // (1 << b)) % 2


def flip(r, b):
    return r + (1 - 2 * bit(r, b)) * (1 << b)


def orders(R):
    high = list(range(1, R.bit_length() - 1))
    return (high, high[::-1])


def subsets(bits):
    out = [0]
    for b in bits:
        out = out + [v + (1 << b) for v in out]
    return out


def greet(R, T, r, t):
    barrier = pltpu.get_barrier_semaphore()
    peers = [(flip(r, b), t) for b in range(R.bit_length() - 1)]
    peers += [(r, (t + j) % T) for j in range(1, T)]
    for peer in peers:
        pl.semaphore_signal(barrier, inc=1, device_id=peer, device_id_type=pl.DeviceIdType.MESH)
    pl.semaphore_wait(barrier, len(peers))


class Sender:
    def __init__(self, send_sem, recv_sem):
        self.send_sem, self.recv_sem, self.used, self.started = send_sem, recv_sem, 0, []

    def start(self, src, dst, peer):
        copy = pltpu.make_async_remote_copy(
            src_ref=src,
            dst_ref=dst,
            send_sem=self.send_sem.at[self.used],
            recv_sem=self.recv_sem.at[self.used],
            device_id=peer,
            device_id_type=pl.DeviceIdType.MESH,
        )
        copy.start()
        self.used += 1
        self.started.append(copy)
        return copy

    def finish(self):
        for copy in self.started:
            copy.wait_send()


def at_slice(index, h):
    return pl.ds(pl.multiple_of(index * h, 16), h)


def rest_of(r, bits):
    total = 0
    for b in bits:
        total = total + bit(r, b) * (1 << b)
    return total


def pack_weights(which, U, SP, refs, outs):
    EP = refs["wedge"].shape[0] if which == 0 else refs["vsq"].shape[1]
    a, b = outs
    if which == 0:
        a[0:U, :] = refs["square"][0].astype(bf16)
        a[U : 2 * U, :] = refs["square"][1].astype(bf16)
        b[0:U, :] = refs["square"][2].astype(bf16)
        b[U : U + SP, :] = pad_rows(refs["wedge"][...], SP).astype(bf16)
        b[U + SP : U + SP + 16, :] = refs["vec"][...].astype(bf16)
    else:
        F4 = 4 * U
        a[0:F4, :] = refs["down"][...].astype(bf16)
        a[F4 : F4 + U, :] = refs["square"][3].astype(bf16)
        for c in range(4):
            b[c * U : (c + 1) * U, :] = refs["up"][:, c * D : (c + 1) * D].astype(bf16)
        zero = jnp.zeros((SP - EP, E), f32)
        for lo, row, n, v in (
            (0, F4, U, refs["vin"][0]),
            (256, F4, U, refs["vin"][1]),
            (0, F4 + U, SP, jnp.concatenate([refs["vsq"][0], zero], axis=0)),
            (256, F4 + U, SP, jnp.concatenate([refs["vsq"][1], zero], axis=0)),
            (0, F4 + U + SP, SP, jnp.concatenate([refs["vsq"][2], zero], axis=0)),
        ):
            b[row : row + n, lo : lo + E] = v.astype(bf16)


def pad_rows(v, n):
    return jnp.concatenate([v, jnp.zeros((n - v.shape[0], v.shape[1]), v.dtype)], axis=0)


def gather_body(which, R, T, names, *refs):
    n = len(names)
    ins = dict(zip(names, refs[:n]))
    outs = refs[n : n + 2]
    packs = refs[n + 2 : n + 4]
    own_sem, send_sem, recv_sem = refs[n + 4 :]
    U, SP, _, _ = place(R, T)
    r, t = lax.axis_index("res"), lax.axis_index("tp")
    greet(R, T, r, t)
    for p in packs:
        p[...] = jnp.zeros_like(p)
    pack_weights(which, U, SP, ins, packs)
    own = []
    for i in range(2):
        copy = pltpu.make_async_copy(packs[i], outs[i].at[t], own_sem.at[i])
        copy.start()
        own.append(copy)
    sender = Sender(send_sem, recv_sem)
    others = [(t + j) % T for j in range(1, T)]
    hs = [p.shape[0] // R for p in packs]
    waiting = []
    for i in range(2):
        mine = at_slice(r, hs[i])
        waiting.append(
            [sender.start(packs[i].at[mine], outs[i].at[t, mine], (r, o)) for o in others]
        )
    paths = [order + [0] for order in orders(R)]
    nbits = R.bit_length() - 1
    for step in range(nbits):
        for i in range(2):
            for copy in waiting[i]:
                copy.wait_recv()
            b = paths[i][step]
            have = paths[i][:step]
            fixed = rest_of(r, [c for c in range(nbits) if c not in have])
            peer = (flip(r, b), t)
            for s in subsets(have):
                where = at_slice(fixed + s, hs[i])
                for o in others:
                    place_ = outs[i].at[o, where]
                    waiting[i].append(sender.start(place_, place_, peer))
            waiting[i] = waiting[i][-len(subsets(have)) * len(others) :]
    for i in range(2):
        for copy in waiting[i]:
            copy.wait_recv()
    sender.finish()
    for copy in own:
        copy.wait()


def gather_weights(which, R, T, ins):
    names = sorted(ins)
    _, _, _, sizes = place(R, T)
    sizes = sizes[2 * which : 2 * which + 2]
    count = 2 * (T - 1) * R
    return pl.pallas_call(
        functools.partial(gather_body, which, R, T, names),
        in_specs=[pl.BlockSpec(memory_space=pltpu.VMEM)] * len(names),
        out_specs=[pl.BlockSpec(memory_space=pl.ANY)] * 2,
        out_shape=[jax.ShapeDtypeStruct((T, n, D), bf16) for n in sizes],
        scratch_shapes=[pltpu.VMEM((n, D), bf16) for n in sizes]
        + [
            pltpu.SemaphoreType.DMA((2,)),
            pltpu.SemaphoreType.DMA((count,)),
            pltpu.SemaphoreType.DMA((count,)),
        ],
        compiler_params=pltpu.CompilerParams(
            vmem_limit_bytes=VMEM_LIMIT, collective_id=1 + which, has_side_effects=True
        ),
        name="gather_weights",
        cost_estimate=pl.CostEstimate(flops=0, bytes_accessed=60 << 20, transcendentals=0),
    )(*[ins[k] for k in names])


def pack_grads(which, U, SP, T, refs, outs):
    a, b = outs
    for t in range(T):
        sl = slice(t * U, (t + 1) * U)
        EP = E // T
        se = slice(t * EP, (t + 1) * EP)
        if which == 0:
            a[t, 0:U, :] = refs["dws"][0, sl, :].astype(bf16)
            a[t, U : 2 * U, :] = refs["dws"][1, sl, :].astype(bf16)
            b[t, 0:U, :] = refs["dw2"][sl, :].astype(bf16)
            b[t, U : U + SP, :] = pad_rows(refs["dwe"][se, :], SP).astype(bf16)
            b[t, U + SP : U + SP + 16, :] = refs["vec"][t].astype(bf16)
        else:
            F4 = 4 * U
            a[t, 0:F4, :] = refs["ddown"][t * F4 : (t + 1) * F4, :].astype(bf16)
            a[t, F4 : F4 + U, :] = refs["dw3"][sl, :].astype(bf16)
            for c in range(4):
                b[t, c * U : (c + 1) * U, :] = refs["dup"][sl, c * D : (c + 1) * D].astype(bf16)
            zero = jnp.zeros((SP - EP, E), f32)
            for lo, row, n, v in (
                (0, F4, U, refs["dvin"][0, sl, :]),
                (256, F4, U, refs["dvin"][1, sl, :]),
                (0, F4 + U, SP, jnp.concatenate([refs["dvsq"][0, se, :], zero], axis=0)),
                (256, F4 + U, SP, jnp.concatenate([refs["dvsq"][1, se, :], zero], axis=0)),
                (0, F4 + U + SP, SP, jnp.concatenate([refs["dvsq"][2, se, :], zero], axis=0)),
            ):
                b[t, row : row + n, lo : lo + E] = v.astype(bf16)


def reduce_body(which, R, T, names, *refs):
    n = len(names)
    ins = dict(zip(names, refs[:n]))
    outs = refs[n : n + 2]
    sqo = refs[n + 2]
    bufs = refs[n + 3 : n + 5]
    lands = refs[n + 5 : n + 7]
    zlands = refs[n + 7 : n + 9]
    sq_land, send_sem, recv_sem = refs[n + 9 :]
    U, SP, _, _ = place(R, T)
    r, t = lax.axis_index("res"), lax.axis_index("tp")
    greet(R, T, r, t)
    for p in bufs:
        p[...] = jnp.zeros_like(p)
    pack_grads(which, U, SP, T, ins, bufs)
    sender = Sender(send_sem, recv_sem)
    nbits = R.bit_length() - 1
    hs = [p.shape[1] // R for p in bufs]
    paths = [[0] + order for order in orders(R)]
    used = [0, 0]
    waiting = [[], []]

    def halve(i, step):
        b, done = paths[i][step], paths[i][:step]
        left = [c for c in range(nbits) if c not in done and c != b]
        fixed = rest_of(r, done)
        peer = (flip(r, b), t)
        waiting[i] = []
        for s in subsets(left):
            land = lands[i].at[used[i]]
            give = at_slice(fixed + (1 - bit(r, b)) * (1 << b) + s, hs[i])
            keep = at_slice(fixed + bit(r, b) * (1 << b) + s, hs[i])
            copy = sender.start(bufs[i].at[:, give, :], land, peer)
            waiting[i].append((copy, used[i], keep))
            used[i] += 1

    def take(i):
        for copy, slot, keep in waiting[i]:
            copy.wait_recv()
            bufs[i][:, keep, :] = (
                bufs[i][:, keep, :].astype(f32) + lands[i][slot].astype(f32)
            ).astype(bf16)

    for step in range(nbits):
        for i in range(2):
            if step:
                take(i)
            halve(i, step)
    for i in range(2):
        take(i)
        mine = at_slice(r, hs[i])
        waiting[i] = [
            sender.start(bufs[i].at[(t + j) % T, mine, :], zlands[i].at[j], (r, (t + j) % T))
            for j in range(1, T)
        ]
    for i in range(2):
        mine = at_slice(r, hs[i])
        total = bufs[i][t, mine, :].astype(f32)
        for j, copy in enumerate(waiting[i]):
            copy.wait_recv()
            total = total + zlands[i][j + 1].astype(f32)
        outs[i][mine, :] = total.astype(bf16)
        waiting[i] = []
    paths = [p[::-1] for p in paths]
    for step in range(nbits):
        for i in range(2):
            for copy in waiting[i]:
                copy.wait_recv()
            b, have = paths[i][step], paths[i][:step]
            fixed = rest_of(r, [c for c in range(nbits) if c not in have])
            waiting[i] = []
            for s in subsets(have):
                spot = outs[i].at[at_slice(fixed + s, hs[i]), :]
                waiting[i].append(sender.start(spot, spot, (flip(r, b), t)))
    squares = jnp.zeros((8, 128), f32)
    for i in range(2):
        for copy in waiting[i]:
            copy.wait_recv()
        for c in range(0, outs[i].shape[0], 128):
            v = outs[i][c : c + 128, :].astype(f32)
            v = jnp.sum((v * v).reshape(16, 8, D), axis=0)
            squares = squares + sum(v[:, k : k + 128] for k in range(0, D, 128))
    if which == 0:
        squares = squares + ins["sq"][...]
        sq_land[0] = squares
        copies = [
            sender.start(sq_land.at[0], sq_land.at[j], (r, (t + j) % T)) for j in range(1, T)
        ]
        for copy in copies:
            copy.wait_recv()
        total = 0.0
        for k in range(T):
            slot = (t + T - k) % T
            total = total + jnp.sum(sq_land[slot])
        squares = jnp.full((8, 128), jnp.sqrt(total), f32)
    sqo[...] = squares
    sender.finish()


def reduce_grads(which, R, T, ins):
    names = sorted(ins)
    _, _, _, sizes = place(R, T)
    sizes = sizes[2 * which : 2 * which + 2]
    count = 2 * (2 * (R - 1) + T - 1) + T
    vm = pl.BlockSpec(memory_space=pltpu.VMEM)
    return pl.pallas_call(
        functools.partial(reduce_body, which, R, T, names),
        in_specs=[vm] * len(names),
        out_specs=[vm] * 3,
        out_shape=[jax.ShapeDtypeStruct((n, D), bf16) for n in sizes]
        + [jax.ShapeDtypeStruct((8, 128), f32)],
        scratch_shapes=[pltpu.VMEM((T, n, D), bf16) for n in sizes]
        + [pltpu.VMEM((R - 1, T, n // R, D), bf16) for n in sizes]
        + [pltpu.VMEM((T, n // R, D), bf16) for n in sizes]
        + [
            pltpu.VMEM((T, 8, 128), f32),
            pltpu.SemaphoreType.DMA((count,)),
            pltpu.SemaphoreType.DMA((count,)),
        ],
        compiler_params=pltpu.CompilerParams(
            vmem_limit_bytes=VMEM_LIMIT, collective_id=3 + which, has_side_effects=True
        ),
        name="reduce_grads",
        cost_estimate=pl.CostEstimate(flops=0, bytes_accessed=60 << 20, transcendentals=0),
    )(*[ins[k] for k in names])


def exchange(rows):
    return lax.all_to_all(rows, ("res", "tp"), split_axis=0, concat_axis=0, tiled=True)


def shards(
    node_feats, edge_feats, slot_index, send_rows, res_mask, chain_ids, node_upstream, edge_upstream,
    *state,
):
    masters, firsts, seconds = state[0:7], state[7:14], state[14:21]
    MB, N, K, _ = edge_feats.shape
    devs = send_rows.shape[2]
    S = devs * send_rows.shape[3]
    R, T = lax.axis_size("res"), lax.axis_size("tp")
    U, SP, EP, _ = place(R, T)
    named = dict(zip(("square", "wedge", "up", "down", "vin", "vsq", "vec"), masters))
    part = masters[6].shape[0]
    named["vec"] = jnp.pad(masters[6], (0, 16 * D - part)).reshape(16, D)
    l0, l1 = gather_weights(0, R, T, {k: named[k] for k in ("square", "wedge", "vec")})
    m0, m1 = gather_weights(1, R, T, {k: named[k] for k in ("square", "up", "down", "vin", "vsq")})
    vec = l1[:, U + SP : U + SP + 16, :].reshape(T, 16 * D)[:, :part].reshape(-1).astype(f32)
    rows = jnp.pad(vec[: 11 * D].reshape(11, D), ((0, 5), (0, 0)))
    c4 = jnp.pad(vec[11 * D : 11 * D + F].reshape(1, F), ((0, 7), (0, 0)))
    rowe = jnp.pad(vec[11 * D + F :].reshape(3, E), ((0, 5), (0, 0)))

    ef = jnp.transpose(edge_feats, (0, 2, 3, 1))
    eup = jnp.transpose(edge_upstream, (0, 2, 3, 1))
    slot = jnp.transpose(slot_index, (2, 0, 1))
    srow = send_rows.reshape(MB, 1, S)
    own = (res_mask * (chain_ids + 1)).astype(f32)
    tags = jnp.broadcast_to(own.astype(bf16)[:, :, None], (MB, N, 128))

    send = node_in(node_feats, srow, tags)
    tabs = [exchange(send[m]) for m in range(MB)]

    mids, fwd, kept = [], [], []
    for m in range(MB):
        a = msg_fwd(m, slot, own, ef, tabs[m], node_feats, l0, l1, rows)
        p1, d1, d2, ps, cnt, vs = a
        fwd.append(a)
        out, x1, a2, q, qd, w, ys, wsend = node_mid(
            m, ps, cnt, node_feats, m0, m1, rows, c4, rowe, srow
        )
        kept.append((out, x1, a2, q, qd, w))
        mids.append((ys, exchange(wsend)))
    before = None
    edges = []
    for m in range(MB):
        ys, tab = mids[m]
        eo, gy1, gys_t, sums, dv, db = edge_net(
            m, slot, fwd[m][5], ef, eup, tab, ys, m1, rowe, before
        )
        before = (dv, db, eo)
        edges.append((gy1, gys_t, exchange(sums.astype(bf16))))
    dvsq, dbe, edge_out = before
    before = None
    backs = []
    for m in range(MB):
        gy1, gys_t, inc = edges[m]
        p1, d1, d2, ps, cnt, vs = fwd[m]
        ho, gx1, *before = node_back(
            m, inc, srow, gys_t, kept[m], node_upstream, m0, m1, rows, ps, cnt, before
        )
        backs.append((ho, gx1))
    dw3, dup, ddown, dvin, vr2, vw = before
    gm0, gm1, sq = reduce_grads(
        1, R, T, {"ddown": ddown, "dw3": dw3, "dup": dup, "dvin": dvin, "dvsq": dvsq}
    )
    before = None
    last = []
    for m in range(MB):
        p1, d1, d2, ps, cnt, vs = fwd[m]
        ego, gzs_t, sums, dw2, dwe, dbm = msg_bwd(
            m, S, slot, vs, ef, eup, p1, d1, d2, edges[m][0], backs[m][0], l1, m1, before
        )
        before = (dw2, dwe, dbm, ego)
        last.append((gzs_t, exchange(sums.astype(bf16))))
    dw2, dwe, dbm, edge_grad = before
    before = None
    node_grads = []
    for m in range(MB):
        gzs_t, inc = last[m]
        ng, *before = node_end(m, inc, srow, gzs_t, node_feats, backs[m][1], l0, rows, before)
        node_grads.append(ng)
    dws, vr1 = before
    vec_grad = jnp.concatenate(
        [
            vr1[0], vr1[1], vr2[0], vr2[1], vr2[2], vr2[3], vr1[2], dbm[1], dbm[0], vr2[4], vr2[5],
            vw[0], vr2[6, :E], dbe[1], dbe[2],
        ]
    )
    vec_grad = jnp.pad(vec_grad.reshape(T, part), ((0, 0), (0, 16 * D - part))).reshape(T, 16, D)
    gl0, gl1, norm = reduce_grads(
        0, R, T, {"dws": dws, "dw2": dw2, "dwe": dwe, "vec": vec_grad, "sq": sq}
    )
    F4 = 4 * U
    total = (
        jnp.stack([gl0[0:U], gl0[U : 2 * U], gl1[0:U], gm0[F4 : F4 + U]]),
        gl1[U : U + EP],
        gm1[0:F4].reshape(4, U, D).transpose(1, 0, 2).reshape(U, F),
        gm0[0:F4],
        jnp.stack([gm1[F4 : F4 + U, 0:E], gm1[F4 : F4 + U, 256 : 256 + E]]),
        jnp.stack(
            [
                gm1[F4 + U : F4 + U + EP, 0:E],
                gm1[F4 + U : F4 + U + EP, 256 : 256 + E],
                gm1[F4 + U + SP : F4 + U + SP + EP, 0:E],
            ]
        ),
        gl1[U + SP : U + SP + 16].reshape(-1)[:part],
    )
    grad_norm = norm[0, 0]
    scale = clip_norm / jnp.maximum(grad_norm, clip_norm)
    first_fix = 1.0 - beta_first**STEP
    second_fix = 1.0 - beta_second**STEP
    new_w, new_f, new_s = [], [], []
    for i in range(7):
        decay, rate = (decay_rate, learn_rate) if i < 6 else (0.0, vector_rate)
        clipped = total[i].astype(f32) * scale
        nf = beta_first * firsts[i] + (1.0 - beta_first) * clipped
        ns = beta_second * seconds[i] + (1.0 - beta_second) * clipped * clipped
        step = nf / first_fix / (jnp.sqrt(ns / second_fix) + adam_eps)
        new_w.append(masters[i] - rate * (step + decay * masters[i]))
        new_f.append(nf)
        new_s.append(ns)
    return (
        jnp.stack([k[0] for k in kept]),
        jnp.transpose(edge_out, (0, 3, 1, 2)),
        jnp.stack(node_grads),
        jnp.transpose(edge_grad, (0, 3, 1, 2)),
        grad_norm.reshape(1),
        *new_w,
        *new_f,
        *new_s,
    )


def solution(mesh):
    lead = ("res", "tp")
    feats = (
        P(None, lead, None),
        P(None, lead, None, None),
        P(None, lead, None),
        P(None, lead, None, None),
        P(None, lead),
        P(None, lead),
        P(None, lead, None),
        P(None, lead, None, None),
    )
    params = (
        P(None, "tp", None),
        P("tp", None),
        P("tp", None),
        P("tp", None),
        P(None, "tp", None),
        P(None, "tp", None),
        P("tp"),
    )
    node, edge = P(None, lead, None), P(None, lead, None, None)
    return jax.shard_map(
        shards,
        mesh=mesh,
        in_specs=feats + params * 3,
        out_specs=(node, edge, node, edge, P()) + params * 3,
        check_vma=False,
    )
```
